256 devices in a mesh: ctx: 16 (over x, y_lo, core), exp: 16 (over z, y_hi).
Axes of the slice: x: 4, y: 4 (y_hi: 2, y_lo: 2; y = y_hi * 2 + y_lo), z: 8, core: 2. Of those that a mesh axis runs over, the one named last changes fastest.
Arguments:
- queries: bfloat16 [12288, 4096], P('ctx', 'exp'), may hold values from -6 to 6
- keys: bfloat16 [12288, 256], P('ctx'), may hold values from -6 to 6
- values: bfloat16 [12288, 256], P('ctx'), may hold values from -6 to 6
- out_weight: bfloat16 [4096, 2048], P('exp'), may hold values from -0.375 to 0.375
- residual: bfloat16 [12288, 2048], P(('ctx', 'exp')), may hold values from -3 to 3
- norm_gain: float32 [2048], replicated, may hold values from 0.5 to 1.5
- route_ids: int32 [12288, 8], P(('ctx', 'exp')), may hold values from 0 to 127, all different within a row; in each aligned block of 48 rows (0 to 47, 48 to 95, ...) at most 4 rows name the same one
- route_gates: float32 [12288, 8], P(('ctx', 'exp')), may hold values from 0.05 to 0.3
- w_gate: bfloat16 [16, 16, 2048, 384], P('ctx', 'exp'), may hold values from -0.125 to 0.125
- w_up: bfloat16 [16, 16, 2048, 384], P('ctx', 'exp'), may hold values from -0.125 to 0.125
- w_down: bfloat16 [16, 16, 384, 2048], P('ctx', 'exp'), may hold values from -0.21875 to 0.21875
Outputs:
- layer_out: bfloat16 [12288, 2048], P(('ctx', 'exp'))
The draws below stay inside these ranges and needn't reach their ends.
Inputs may be any that keep to these rules, and one draw needn't show every extreme that they name: `route_ids`: in the 48 rows of one device no expert is named more than 4 times, and in every draw some expert is named exactly 4 times there; each row names 8 different experts.
All inputs are finite; a program needn't handle non-finite values.
Results may differ from the reference program's by a relative error of at most 0.02.
Values may be sent and summed in bfloat16 or wider, within the bound.
No kernel may reach another device: no remote copies, remote signals or barrier semaphores. Data moves between devices by JAX's collectives and lax.ppermute only.
A program may use at most 64 MiB of HBM per device.

```python
import math
import jax
import jax.numpy as jnp
import numpy as np
from jax import lax

D = 2048
FF = 768
HEAD_WIDTH = 128
QUERY_HEADS = 32
KEY_VALUE_HEADS = 2
TOP = 8
TOK_DEV = 48
SEQUENCE_LENGTH = 12288
EXP_OWN = 8
EXPERTS = 128
MOST = 4
N_CTX = 16
N_EXP = 16


def draw_queries(key, part):
    key = jax.random.fold_in(key, 7)
    limit = 6.0
    base_offset = 1.2 * jax.random.normal(key, (SEQUENCE_LENGTH, QUERY_HEADS * HEAD_WIDTH))
    return jnp.clip(base_offset, -limit, limit).astype(jnp.bfloat16)


def draw_keys(key, part):
    key = jax.random.fold_in(key, 13)
    limit = 6.0
    base_offset = 1.2 * jax.random.normal(key, (SEQUENCE_LENGTH, KEY_VALUE_HEADS * HEAD_WIDTH))
    return jnp.clip(base_offset, -limit, limit).astype(jnp.bfloat16)


def block_scale(rng, dims, cuts, least, top_value):
    def one(position, shards_of):
        heights = jax.random.uniform(jax.random.fold_in(jax.random.fold_in(rng, 6), position), (shards_of,), jnp.float32, least / len(cuts), top_value / len(cuts))
        return jnp.repeat(jnp.exp(heights), dims[position] // shards_of).reshape((-1,) + (1,) * (len(dims) - position - 1))

    loudness = one(*cuts[0])
    for cut in cuts[1:]:
        loudness = loudness * one(*cut)
    return loudness


def deal_out(stream_key, own, number, rows, number_of, top, reach, slope):
    order = jax.random.permutation(stream_key, number_of)
    crowded, usual = load_shares(number_of, rows * top, reach, slope, True), load_shares(number_of, rows * top, reach, slope, False)
    places = jnp.arange(number_of)

    def named(sizes, offset_by):
        used = int((sizes > 0).sum())
        fixed = max(1, used // 4)
        passed = fixed + (places - fixed + offset_by * (used - fixed)) % max(1, number_of - fixed)
        return jnp.zeros((number_of,), jnp.int32).at[order[jnp.where(places < fixed, places, passed)]].set(jnp.asarray(sizes, jnp.int32))

    sizes = jnp.where(number % 4 == 0, named(crowded, number // 4), named(usual, number - number // 4 - 1))
    mixed = jax.random.permutation(jax.random.fold_in(own, 3), number_of)
    giver, taker = mixed[0:number_of // 2 * 2:2], mixed[1:number_of // 2 * 2:2]
    margin = jnp.minimum(sizes[giver] - 1, reach - sizes[taker]) // 2
    margin = jnp.where((giver == order[0]) | (taker == order[0]) | (sizes[taker] == 0), 0, jnp.maximum(margin, 0))
    passed = jax.random.randint(jax.random.fold_in(own, 4), (number_of // 2,), 0, 1 << 20) % (margin + 1)
    sizes = sizes.at[giver].add(-passed).at[taker].add(passed)
    items = jnp.searchsorted(jnp.cumsum(sizes), jnp.arange(rows * top), side="right").astype(jnp.int32)
    grid = items.reshape(top, rows).T
    grid = grid[jax.random.permutation(jax.random.fold_in(own, 1), rows)]
    offset_by = jax.random.randint(jax.random.fold_in(own, 2), (rows, 1), 0, top)
    return jnp.take_along_axis(grid, (jnp.arange(top)[None, :] + offset_by) % top, axis=1)


def load_shares(count, total, reach, lean, full):
    loads = [(1 << 20) // math.isqrt(rank ** lean) + 1 for rank in range(1, count + 1)]
    largest = reach if full else min(reach, max(-(-total // count), total * loads[0] // sum(loads)))
    least = 1 if total - largest >= count - 1 else 0
    counts, rest = [largest] + [least] * (count - 1), total - largest - least * (count - 1)
    while rest > 0:
        movable = [i for i in range(1, count) if counts[i] < largest] or [i for i in range(1, count) if counts[i] < reach]
        mass, remaining = sum([loads[i] for i in movable]), rest
        for i in movable:
            addition = min(reach - counts[i], max(1, remaining * loads[i] // mass), rest)
            counts[i] = counts[i] + addition
            rest = rest - addition
    return np.array(counts)


def normal_values(key, extent, scale, most, cuts=(), held_as=jnp.bfloat16):
    values = scale * jax.random.normal(key, extent, jnp.float32)
    if cuts:
        values = values * block_scale(key, extent, cuts, -0.22, 0.18)
    return jnp.clip(values, -most, most).astype(held_as)


def setup_inputs(seed: int = 0) -> dict:
    streams_of = jax.random.split(jax.random.key(seed), 12)
    queries = draw_queries(jax.random.fold_in(streams_of[11], 71), 0)
    keys = draw_keys(jax.random.fold_in(streams_of[11], 71), 0)
    values = normal_values(streams_of[2], (SEQUENCE_LENGTH, KEY_VALUE_HEADS * HEAD_WIDTH), 1.0, 6.0, ((0, 16),))
    out_weight = normal_values(streams_of[3], (QUERY_HEADS * HEAD_WIDTH, D), (QUERY_HEADS * HEAD_WIDTH // 16) ** -0.5, 0.375, ((0, 16),))
    residual = normal_values(streams_of[4], (SEQUENCE_LENGTH, D), 0.5, 3.0, ((0, 256),))
    norm_gain = jnp.clip(1.0 + 0.1 * jax.random.normal(streams_of[5], (D,), jnp.float32), 0.5, 1.5)
    route_ids_keys = jax.random.split(jax.random.fold_in(streams_of[6], 1), SEQUENCE_LENGTH // TOK_DEV)
    route_ids_turns = jax.random.permutation(jax.random.fold_in(streams_of[6], 3), SEQUENCE_LENGTH // TOK_DEV)
    route_ids = jax.vmap(lambda own, number: deal_out(jax.random.fold_in(streams_of[6], 2), own, number, TOK_DEV, EXPERTS, TOP, MOST, 2))(route_ids_keys, route_ids_turns).reshape((SEQUENCE_LENGTH, TOP))
    route_gates = jnp.clip(jnp.exp(math.log(0.3) - 1.7917595 * jax.random.uniform(streams_of[7], (SEQUENCE_LENGTH, TOP), jnp.float32) ** block_scale(streams_of[7], (SEQUENCE_LENGTH, TOP), ((0, 256),), -0.2, 0.2)), 0.05, 0.3)
    w_gate = normal_values(streams_of[8], (2 * EXP_OWN, N_EXP, D, FF // 2), D ** -0.5, 0.125, ((0, 16), (1, 16)))
    w_up = normal_values(streams_of[9], (2 * EXP_OWN, N_EXP, D, FF // 2), D ** -0.5, 0.125, ((0, 16), (1, 16)))
    w_down = normal_values(streams_of[10], (2 * EXP_OWN, N_EXP, FF // 2, D), FF ** -0.5, 0.21875, ((0, 16), (1, 16)))
    return {"queries": queries, "keys": keys, "values": values, "out_weight": out_weight, "residual": residual, "norm_gain": norm_gain, "route_ids": route_ids, "route_gates": route_gates, "w_gate": w_gate, "w_up": w_up, "w_down": w_down}


def attend_rows(queries, keys, values):
    group_length = QUERY_HEADS // KEY_VALUE_HEADS
    score_scale = 1.0 / math.sqrt(HEAD_WIDTH)
    block_row_count = math.gcd(SEQUENCE_LENGTH, 512)
    key_head_stack = keys.astype(jnp.float32).reshape(SEQUENCE_LENGTH, KEY_VALUE_HEADS, HEAD_WIDTH)
    value_head_stack = values.astype(jnp.float32).reshape(SEQUENCE_LENGTH, KEY_VALUE_HEADS, HEAD_WIDTH)

    def one_block(row_start):
        query_block = lax.dynamic_slice_in_dim(queries, row_start, block_row_count, 0)
        query_block = query_block.astype(jnp.float32).reshape(block_row_count, KEY_VALUE_HEADS, group_length, HEAD_WIDTH)
        q_pos = row_start + jnp.arange(block_row_count, dtype=jnp.int32)
        k_pos = jnp.arange(SEQUENCE_LENGTH, dtype=jnp.int32)
        allowed = k_pos[None, :] <= q_pos[:, None]
        results = []
        for key_value_index in range(KEY_VALUE_HEADS):
            scores = jnp.einsum('qhd,kd->hqk', query_block[:, key_value_index], key_head_stack[:, key_value_index]) * score_scale
            scores = jnp.where(allowed[None], scores, -jnp.inf)
            top_score = lax.optimization_barrier(jnp.max(scores, axis=-1, keepdims=True))
            exp_terms = jnp.exp(scores - top_score)
            totals = lax.optimization_barrier(jnp.sum(exp_terms, axis=-1))
            weights = lax.optimization_barrier(exp_terms.astype(jnp.bfloat16)).astype(jnp.float32)
            summed = jnp.einsum('hqk,kd->qhd', weights, value_head_stack[:, key_value_index])
            results.append(summed / jnp.transpose(totals)[:, :, None])
        joined = jnp.concatenate(results, axis=1)
        return joined.reshape(block_row_count, QUERY_HEADS * HEAD_WIDTH).astype(jnp.bfloat16)
    row_starts = jnp.arange(SEQUENCE_LENGTH // block_row_count, dtype=jnp.int32) * block_row_count
    return lax.map(one_block, row_starts).reshape(SEQUENCE_LENGTH, QUERY_HEADS * HEAD_WIDTH)

def reference(queries, keys, values, out_weight, residual, norm_gain, route_ids, route_gates, w_gate, w_up, w_down):
    attended = attend_rows(queries, keys, values)
    group_width = QUERY_HEADS * HEAD_WIDTH // N_EXP

    def add_group(group_index, running):
        columns = lax.dynamic_slice_in_dim(attended, group_index * group_width, group_width, 1)
        rows_of_w = lax.dynamic_slice_in_dim(out_weight, group_index * group_width, group_width, 0)
        term = jnp.dot(columns, rows_of_w, preferred_element_type=jnp.float32)
        return running + lax.optimization_barrier(term.astype(jnp.bfloat16)).astype(jnp.float32)
    mixed = lax.fori_loop(0, N_EXP, add_group, residual.astype(jnp.float32))
    mean_square = lax.optimization_barrier(jnp.mean(mixed * mixed, axis=-1, keepdims=True))
    normed = (mixed * lax.rsqrt(mean_square + 1e-06) * norm_gain).astype(jnp.bfloat16)
    flat_ids = route_ids.reshape(-1)
    flat_gates = route_gates.reshape(-1)
    capacity = N_CTX * N_EXP * MOST

    def expert_step(running, expert):
        owner = expert // EXP_OWN
        local_index = expert % EXP_OWN
        hits = flat_ids == expert
        picks = jnp.nonzero(hits, size=capacity, fill_value=0)[0].astype(jnp.int32)
        live = (jnp.arange(capacity) < jnp.sum(hits)).astype(jnp.float32)
        token_rows = picks // TOP
        inputs = normed[token_rows]
        halves = []
        for half_index in range(2):
            piece = 2 * local_index + half_index
            gate_part = jnp.dot(inputs, w_gate[piece, owner], preferred_element_type=jnp.float32)
            up_part = jnp.dot(inputs, w_up[piece, owner], preferred_element_type=jnp.float32)
            hidden = (jax.nn.silu(gate_part) * up_part).astype(jnp.bfloat16)
            half_out = jnp.dot(hidden, w_down[piece, owner], preferred_element_type=jnp.float32)
            halves.append(lax.optimization_barrier(half_out.astype(jnp.bfloat16)).astype(jnp.float32))
        expert_out = lax.optimization_barrier((halves[0] + halves[1]).astype(jnp.bfloat16)).astype(jnp.float32)
        contrib = expert_out * (flat_gates[picks] * live)[:, None]
        return (running.at[token_rows].add(contrib), None)
    moe_sum, _ = lax.scan(expert_step, jnp.zeros((SEQUENCE_LENGTH, D), jnp.float32), jnp.arange(EXPERTS, dtype=jnp.int32))
    return (mixed + moe_sum).astype(jnp.bfloat16)
```

```python
import functools
import math

import jax
import jax.numpy as jnp
import numpy as np
from jax import lax
from jax.experimental import pallas as pl
from jax.experimental.pallas import tpu as pltpu
from jax.sharding import PartitionSpec as P

HEAD = 128
NEG = -1e30
BF = jnp.bfloat16
F32 = jnp.float32
VMEM = pltpu.VMEM
MIB = 1 << 20


def params(mib):
    return pltpu.CompilerParams(vmem_limit_bytes=mib * MIB)


def vmem_specs(count):
    return [pl.BlockSpec(memory_space=VMEM)] * count


def mm(a, b):
    return jnp.dot(a, b, preferred_element_type=F32)


def attend_tile(s, keys2, values1, pos_ref, q_scr, m_ref, l_ref, a_ref, masked, tile):
    rows, width = q_scr.shape[1], keys2.shape[0]
    for start in range(0, rows, tile):
        sl = pl.ds(start, tile)
        scores = lax.dot_general(
            q_scr[s, sl, :], keys2, (((1,), (1,)), ((), ())), preferred_element_type=F32
        )
        if masked:
            k_pos = lax.broadcasted_iota(jnp.int32, (tile, width), 1)
            scores = jnp.where(k_pos <= pos_ref[s, sl, :], scores, NEG)
        m_old = m_ref[s, sl, :]
        m_new = jnp.maximum(m_old, jnp.max(scores, axis=1, keepdims=True))
        terms = jnp.exp2(scores - jnp.concatenate([m_new] * (width // 128), axis=1))
        update = mm(terms.astype(BF), values1)
        shrink = jnp.exp2(m_old - m_new)
        a_ref[s, sl, :] = a_ref[s, sl, :] * shrink + update[:, :HEAD]
        l_ref[s, sl, :] = l_ref[s, sl, :] * shrink + update[:, HEAD:]
        m_ref[s, sl, :] = m_new


def attend_kernel(counts, first, last, meta, pos_ref, q_ref, *refs):
    n = len(counts)
    kv_refs, refs = refs[:n], refs[n:]
    if not first:
        state_in, refs = refs[:3], refs[3:]
    if last:
        o_ref, q_scr, m_ref, l_ref, a_ref = refs
    else:
        m_ref, l_ref, a_ref, q_scr = refs
    scale = np.float32(math.log2(math.e) / math.sqrt(HEAD))
    for s in range(2):
        for k in range(4):
            for p in range(2):
                q = q_ref[s, k, :, p * HEAD : (p + 1) * HEAD].astype(F32) * scale
                high = q.astype(BF)
                low = (q - high.astype(F32)).astype(BF)
                sl = pl.ds((k * 2 + p) * 96, 96)
                q_scr[s, sl, :HEAD] = high
                q_scr[s, sl, HEAD:] = low
    if first:
        m_ref[...] = jnp.full(m_ref.shape, NEG, F32)
        l_ref[...] = jnp.zeros(l_ref.shape, F32)
        a_ref[...] = jnp.zeros(a_ref.shape, F32)
    else:
        m_ref[...] = state_in[0][...]
        l_ref[...] = state_in[1][...]
        a_ref[...] = state_in[2][...]

    def one_block(kv_ref, i, base):
        block_ctx = meta[base + i]
        sl = pl.ds(pl.multiple_of(i * 768, 768), 768)
        for s in range(2):
            set_ctx = meta[16 + s]

            def run(masked):
                k = kv_ref[sl, :HEAD]
                v = kv_ref[sl, HEAD:]
                keys2 = jnp.concatenate([k, k], axis=1)
                values1 = jnp.concatenate([v, jnp.ones_like(v)], axis=1)
                attend_tile(
                    s, keys2, values1, pos_ref, q_scr, m_ref, l_ref, a_ref, masked, 256
                )

            pl.when(block_ctx < set_ctx)(functools.partial(run, False))
            pl.when(block_ctx == set_ctx)(functools.partial(run, True))

    base = 0
    for kv_ref, count in zip(kv_refs, counts):
        if count == 1:
            one_block(kv_ref, 0, base)
        else:

            def step(i, carry, kv_ref=kv_ref, base=base):
                one_block(kv_ref, i, base)
                return carry

            lax.fori_loop(0, count, step, 0)
        base += count
    if last:
        o_ref[...] = (a_ref[...] / l_ref[...]).astype(BF).reshape(o_ref.shape)


def attend(meta, pos, q, blocks, state, last):
    counts = tuple(b.shape[0] // 768 for b in blocks)
    first = state is None
    state_in = () if first else state
    state_shape = jax.ShapeDtypeStruct((2, 768, HEAD), F32)
    q_scr = VMEM((2, 768, 2 * HEAD), BF)
    if last:
        out_shape = jax.ShapeDtypeStruct((2, 8, 96, HEAD), BF)
        scratch = [q_scr] + [VMEM((2, 768, HEAD), F32)] * 3
        out_specs = pl.BlockSpec(memory_space=VMEM)
    else:
        out_shape = [state_shape] * 3
        scratch = [q_scr]
        out_specs = vmem_specs(3)
    units = sum(counts) * 17 / 16
    return pl.pallas_call(
        functools.partial(attend_kernel, counts, first, last),
        out_shape=out_shape,
        in_specs=[pl.BlockSpec(memory_space=pltpu.SMEM)]
        + vmem_specs(2 + len(blocks) + len(state_in)),
        out_specs=out_specs,
        scratch_shapes=scratch,
        compiler_params=params(40),
        cost_estimate=pl.CostEstimate(
            flops=int(units * 1.3e9), bytes_accessed=8 << 20, transcendentals=int(units * 600000)
        ),
        name="attend",
    )(meta, pos, q, *blocks, *state_in)


def project_kernel(meta, att_ref, w_own, w1, w2, w3, x1, x2, x3, own_ref, o1, o2, o3, acc):
    k, p = meta[0], meta[1]

    def rows(head):
        return jnp.concatenate([att_ref[0, head], att_ref[1, head]], axis=0)

    for c0 in range(0, 2048, 512):
        cols = pl.ds(c0, 512)
        total = mm(rows(2 * k), w_own[0:HEAD, cols]) + mm(rows(2 * k + 1), w_own[HEAD:, cols])
        for j, (mine, other) in enumerate(((w1, x1), (w2, x2), (w3, x3))):
            peer = 2 * (k ^ (j + 1))
            total = total + mm(rows(peer + p), mine[:, cols])
            total = total + mm(rows(peer + 1 - p), other[:, cols])
        for i in range(4):
            acc[i, :, cols] = total[48 * i : 48 * i + 48]
    own_ref[...] = acc[meta[2]]
    o1[...] = acc[meta[3]].astype(BF)
    o2[...] = acc[meta[4]].astype(BF)
    o3[...] = acc[meta[5]].astype(BF)


def project(meta, att, weights):
    sent = jax.ShapeDtypeStruct((48, 2048), BF)
    return pl.pallas_call(
        project_kernel,
        out_shape=[jax.ShapeDtypeStruct((48, 2048), F32), sent, sent, sent],
        in_specs=[pl.BlockSpec(memory_space=pltpu.SMEM)] + vmem_specs(1 + len(weights)),
        out_specs=vmem_specs(4),
        scratch_shapes=[VMEM((4, 48, 2048), F32)],
        compiler_params=params(24),
        cost_estimate=pl.CostEstimate(
            flops=2 * 192 * 1024 * 2048, bytes_accessed=6 << 20, transcendentals=0
        ),
        name="project",
    )(meta, att, *weights)


def iota(shape, dim):
    return lax.broadcasted_iota(jnp.int32, shape, dim)


def row_fields(row):
    device = row >> 3
    ctx = device >> 4
    expert = ((device & 15) << 3) | (ctx >> 1)
    rank = ((ctx & 1) << 1) | ((row >> 2) & 1)
    return expert, rank, row & 3


def route_kernel(ids_ref, ids_t_ref, gates_ref, send_ref, high_ref, low_ref):
    ids, ids_t, gates = ids_ref[...], ids_t_ref[...], gates_ref[...]
    expert_lane = iota((48, 128), 1)
    named = jnp.zeros((48, 128), F32)
    gate = jnp.zeros((48, 128), F32)
    expert_row = iota((128, 48), 0)
    named_t = jnp.zeros((128, 48), F32)
    for k in range(8):
        hit = ids[:, k : k + 1] == expert_lane
        named = named + jnp.where(hit, 1.0, 0.0)
        gate = gate + jnp.where(hit, gates[:, k : k + 1], 0.0)
        named_t = named_t + jnp.where(ids_t[k : k + 1, :] == expert_row, 1.0, 0.0)
    lower = jnp.where(iota((48, 48), 1) <= iota((48, 48), 0), 1.0, 0.0).astype(BF)
    upper = jnp.where(iota((48, 48), 0) <= iota((48, 48), 1), 1.0, 0.0).astype(BF)
    rank = (mm(lower, named.astype(BF)) * named).astype(BF)
    rank_t = (mm(named_t.astype(BF), upper) * named_t).astype(BF)
    high = gate.astype(BF)
    low = (gate - high.astype(F32)).astype(BF)

    expert, want, quarter = row_fields(iota((2048, 128), 0))
    pick = jnp.where(expert == iota((2048, 128), 1), 1.0, 0.0).astype(BF)
    have = mm(pick, rank_t)
    expert, want, quarter = row_fields(iota((2048, 48), 0))
    wanted = (want + 1).astype(F32)
    parts = [jnp.where((have == wanted) & (quarter == q), 1.0, 0.0) for q in range(4)]
    for q in range(4):
        send_ref[:, 48 * q : 48 * q + 48] = parts[q].astype(BF)

    expert, want, quarter = row_fields(iota((128, 2048), 1))
    pick = jnp.where(expert == iota((128, 2048), 0), 1.0, 0.0).astype(BF)
    have = mm(rank, pick)
    got_high, got_low = mm(high, pick), mm(low, pick)
    expert, want, quarter = row_fields(iota((48, 2048), 1))
    live = have == (want + 1).astype(F32)
    for q in range(4):
        here = live & (quarter == q)
        sl = pl.ds(48 * q, 48)
        high_ref[sl, :] = jnp.where(here, got_high, 0.0).astype(BF)
        low_ref[sl, :] = jnp.where(here, got_low, 0.0).astype(BF)


def route(ids, gates):
    back = jax.ShapeDtypeStruct((192, 2048), BF)
    return pl.pallas_call(
        route_kernel,
        out_shape=[jax.ShapeDtypeStruct((2048, 192), BF), back, back],
        in_specs=vmem_specs(3),
        out_specs=vmem_specs(3),
        compiler_params=params(32),
        cost_estimate=pl.CostEstimate(
            flops=400 << 20, bytes_accessed=3 << 20, transcendentals=0
        ),
        name="route",
    )(ids, ids.T, gates)


def dispatch_kernel(residual, own, r1, r2, r3, gain, send, mixed_ref, out_ref, stack):
    mixed = residual[...].astype(F32) + own[...]
    mixed = mixed + r1[...].astype(F32) + r2[...].astype(F32) + r3[...].astype(F32)
    mixed_ref[...] = mixed
    mean_square = jnp.mean(mixed * mixed, axis=-1, keepdims=True)
    normed = (mixed * lax.rsqrt(mean_square + 1e-06) * gain[...]).astype(BF)
    for q in range(4):
        stack[48 * q : 48 * q + 48, :] = normed[:, 512 * q : 512 * q + 512]

    def step(i, carry):
        sl = pl.ds(pl.multiple_of(i * 256, 256), 256)
        out_ref[sl, :] = mm(send[sl, :], stack[...]).astype(BF)
        return carry

    lax.fori_loop(0, 8, step, 0)


def dispatch(residual, own, received, gain, send):
    return pl.pallas_call(
        dispatch_kernel,
        out_shape=[
            jax.ShapeDtypeStruct((48, 2048), F32),
            jax.ShapeDtypeStruct((2048, 512), BF),
        ],
        in_specs=vmem_specs(7),
        out_specs=vmem_specs(2),
        scratch_shapes=[VMEM((192, 512), BF)],
        compiler_params=params(24),
        name="dispatch",
    )(residual, own, *received, gain, send)


def combine_kernel(mixed, high, low, results, out_ref):
    total = mm(high[...], results[...]) + mm(low[...], results[...])
    for q in range(4):
        cols = pl.ds(512 * q, 512)
        out_ref[:, cols] = (mixed[:, cols] + total[48 * q : 48 * q + 48]).astype(BF)


def combine(mixed, high, low, results):
    return pl.pallas_call(
        combine_kernel,
        out_shape=jax.ShapeDtypeStruct((48, 2048), BF),
        in_specs=vmem_specs(4),
        out_specs=pl.BlockSpec(memory_space=VMEM),
        compiler_params=params(24),
        name="combine",
    )(mixed, high, low, results)


def expert_kernel(
    rows_ref, g0, u0, d0, g1, u1, d1, out_ref, x_scr, y_scr, gate_scr, up_scr, down_scr, sems
):
    copies = []
    for i, (g, u, d) in enumerate(((g0, u0, d0), (g1, u1, d1))):
        copies.append(
            (
                pltpu.make_async_copy(g, gate_scr.at[i], sems.at[3 * i]),
                pltpu.make_async_copy(u, up_scr.at[i], sems.at[3 * i + 1]),
                pltpu.make_async_copy(d, down_scr.at[i], sems.at[3 * i + 2]),
            )
        )
    for trio in copies:
        for copy in trio:
            copy.start()
    to_row, from_col = iota((256, 256), 0), iota((256, 256), 1)
    sort = jnp.where(from_col == ((to_row & 63) << 2) + (to_row >> 6), 1.0, 0.0).astype(BF)
    unsort = jnp.where(to_row == ((from_col & 63) << 2) + (from_col >> 6), 1.0, 0.0).astype(BF)

    def spread(b, carry):
        sl = pl.ds(pl.multiple_of(b * 256, 256), 256)
        tokens = pl.ds(pl.multiple_of(b * 64, 64), 64)
        block = mm(sort, rows_ref[sl, :]).astype(BF)
        for q in range(4):
            x_scr[tokens, 512 * q : 512 * q + 512] = block[64 * q : 64 * q + 64]
        return carry

    lax.fori_loop(0, 8, spread, 0)
    for i in range(2):
        for copy in copies[i]:
            copy.wait()

        def half(t, carry, i=i):
            tokens = pl.ds(pl.multiple_of(t * 256, 256), 256)
            x = x_scr[tokens, :]
            gate = mm(x, gate_scr[i])
            up = mm(x, up_scr[i])
            hidden = (gate / (1.0 + jnp.exp(-gate)) * up).astype(BF)
            for c0 in range(0, 2048, 512):
                cols = pl.ds(c0, 512)
                part = mm(hidden, down_scr[i, :, cols])
                if i == 0:
                    y_scr[tokens, cols] = part
                else:
                    y_scr[tokens, cols] = y_scr[tokens, cols] + part
            return carry

        lax.fori_loop(0, 2, half, 0)

    def gather(b, carry):
        sl = pl.ds(pl.multiple_of(b * 256, 256), 256)
        tokens = pl.ds(pl.multiple_of(b * 64, 64), 64)
        block = jnp.concatenate(
            [y_scr[tokens, 512 * q : 512 * q + 512] for q in range(4)], axis=0
        )
        out_ref[sl, :] = mm(unsort, block.astype(BF)).astype(BF)
        return carry

    lax.fori_loop(0, 8, gather, 0)


def experts(rows, weights):
    return pl.pallas_call(
        expert_kernel,
        out_shape=jax.ShapeDtypeStruct((2048, 512), BF),
        in_specs=vmem_specs(1) + [pl.BlockSpec(memory_space=pl.ANY)] * 6,
        out_specs=pl.BlockSpec(memory_space=VMEM),
        scratch_shapes=[
            VMEM((512, 2048), BF),
            VMEM((512, 2048), F32),
            VMEM((2, 2048, 384), BF),
            VMEM((2, 2048, 384), BF),
            VMEM((2, 384, 2048), BF),
            pltpu.SemaphoreType.DMA((6,)),
        ],
        compiler_params=params(40),
        name="experts",
    )(rows, *weights)


def along_ctx(x, source_of):
    return lax.ppermute(x, "ctx", [(source_of(c), c) for c in range(16)])


def along_exp(x, flip):
    return lax.ppermute(x, "exp", [(e ^ flip, e) for e in range(16)])


def along_both(x, mirror, flip):
    pairs = [
        (c * 16 + e, ((15 - c) if mirror else c) * 16 + (e ^ flip))
        for c in range(16)
        for e in range(16)
    ]
    return lax.ppermute(x, ("ctx", "exp"), pairs)


def local(
    queries,
    keys,
    values,
    out_weight,
    residual,
    norm_gain,
    route_ids,
    route_gates,
    w_gate,
    w_up,
    w_down,
):
    c = lax.axis_index("ctx")
    e = lax.axis_index("exp")
    core, g, k = c % 2, e // 4, e % 4
    high_ctx = (c >= 8).astype(jnp.int32)
    pair = g // 2
    ctx_low, ctx_high = jnp.minimum(c, 15 - c), jnp.maximum(c, 15 - c)

    kv_head = e // 8
    own = jnp.concatenate(
        [
            lax.dynamic_slice_in_dim(keys, kv_head * HEAD, HEAD, 1),
            lax.dynamic_slice_in_dim(values, kv_head * HEAD, HEAD, 1),
        ],
        axis=1,
    )

    def swap(x):
        return along_ctx(x, lambda i: i ^ 1)

    def from_y(x):
        return along_ctx(x, lambda i: i ^ 2)

    def from_x(x, step):
        return along_ctx(x, lambda i: (i + 4 * step) % 16)

    own_s = swap(own)
    n1, n2, n3 = from_x(own, 1), from_x(own, -1), from_y(own)
    s1, s2, s3 = swap(n1), swap(n2), swap(n3)
    n4, n5, n6 = from_x(n1, 1), from_x(n3, -1), from_y(n1)
    s4, s5, s6 = swap(n4), swap(n5), swap(n6)
    n7 = jnp.concatenate(
        [from_y(n4[0:256]), from_x(n6[256:512], 1), from_x(n5[512:768], -1)], axis=0
    )
    s7 = swap(n7)
    x, y = c // 4, (c // 2) % 2

    def ctx_of(dx, dy, dp):
        return ((x + dx) % 4) * 4 + (y ^ dy) * 2 + (core ^ dp)

    near = [(0, 0), (1, 0), (3, 0), (0, 1)]
    far = [(2, 0), (3, 1), (1, 1), (2, 1)]
    order = [ctx_of(*a, 0) for a in near] + [ctx_of(*a, 1) for a in near]
    order += [ctx_of(*a, 0) for a in far] + [ctx_of(*a, 1) for a in far]

    grouped = queries.reshape(2, 2, 4, 48, 256).transpose(0, 2, 1, 3, 4)
    swapped = (pair + high_ctx) % 2
    outgoing = jnp.where(swapped == 0, grouped, grouped[::-1])
    teams = [
        [cc * 16 + gg * 4 + kk for cc in (low, 15 - low) for kk in range(4)]
        for low in range(8)
        for gg in range(4)
    ]
    q = lax.all_to_all(
        outgoing.reshape(8, 96, 256),
        ("ctx", "exp"),
        split_axis=0,
        concat_axis=0,
        tiled=True,
        axis_index_groups=teams,
    ).reshape(2, 4, 96, 256)
    token = jnp.arange(96, dtype=jnp.int32)
    pair_of = jnp.stack([(pair + high_ctx) % 2, (pair + 1 - high_ctx) % 2])
    pos = ((2 * pair_of[:, None] + token[None, :] // 48) * 4 + k) * 48 + token[None, :] % 48
    pos = jnp.broadcast_to(pos[:, None, :], (2, 8, 96)).reshape(2, 768, 1)

    sets = [ctx_low, ctx_high]
    near_meta = jnp.stack(order[:8] + [ctx_low] * 8 + sets).astype(jnp.int32)
    far_meta = jnp.stack(order[8:] + [ctx_low] * 8 + sets).astype(jnp.int32)
    state = attend(near_meta, pos, q, [own, n1, n2, n3, own_s, s1, s2, s3], None, False)
    attended = attend(far_meta, pos, q, [n4, n5, n6, n7, s4, s5, s6, s7], state, True)

    w_part = lax.dynamic_slice_in_dim(out_weight, core * HEAD, HEAD, 0)
    w_near = [along_exp(w_part, flip) for flip in (1, 2, 3)]
    w_other = [swap(w) for w in w_near]
    own_set, odd = high_ctx, g % 2
    meta = jnp.stack(
        [
            k,
            core,
            own_set * 2 + odd,
            own_set * 2 + 1 - odd,
            (1 - own_set) * 2 + odd,
            (1 - own_set) * 2 + 1 - odd,
        ]
    ).astype(jnp.int32)
    mine, t1, t2, t3 = project(meta, attended, [out_weight] + w_near + w_other)
    received = [along_both(t1, False, 4), along_both(t2, True, 8), along_both(t3, True, 12)]

    send, back_high, back_low = route(route_ids, route_gates)
    mixed, rows = dispatch(residual, mine, received, norm_gain[None, :], send)

    own_w = [w_gate[0, 0], w_up[0, 0], w_down[0, 0]]
    other_w = [swap(w) for w in own_w]

    def exchange(v):
        return lax.all_to_all(
            v.reshape(256, 8, 512), ("ctx", "exp"), split_axis=0, concat_axis=0, tiled=True
        ).reshape(2048, 512)

    results = exchange(experts(exchange(rows), own_w + other_w))
    return combine(mixed, back_high, back_low, results)


def solution(mesh):
    placed = (
        P("ctx", "exp"),
        P("ctx", None),
        P("ctx", None),
        P("exp", None),
        P(("ctx", "exp"), None),
        P(),
        P(("ctx", "exp"), None),
        P(("ctx", "exp"), None),
        P("ctx", "exp", None, None),
        P("ctx", "exp", None, None),
        P("ctx", "exp", None, None),
    )
    return jax.shard_map(
        local, mesh=mesh, in_specs=placed, out_specs=P(("ctx", "exp"), None), check_vma=False
    )
```

```python
import functools
import math

import jax
import jax.numpy as jnp
import numpy as np
from jax import lax
from jax.experimental import pallas as pl
from jax.experimental.pallas import tpu as pltpu
from jax.sharding import PartitionSpec as P

HEAD = 128
NEG = -1e30
BF = jnp.bfloat16
F32 = jnp.float32
VMEM = pltpu.VMEM
MIB = 1 << 20


def params(mib):
    return pltpu.CompilerParams(vmem_limit_bytes=mib * MIB)


def vmem_specs(count):
    return [pl.BlockSpec(memory_space=VMEM)] * count


def mm(a, b):
    return jnp.dot(a, b, preferred_element_type=F32)


def attend_tile(keys2, values1, base, q_scr, m_ref, l_ref, a_ref, masked, tile):
    rows, width = q_scr.shape[0], keys2.shape[0]
    for start in range(0, rows, tile):
        sl = pl.ds(start, tile)
        scores = lax.dot_general(
            q_scr[sl, :], keys2, (((1,), (1,)), ((), ())), preferred_element_type=F32
        )
        if masked:
            k_pos = lax.broadcasted_iota(jnp.int32, (tile, width), 1)
            row = start + iota((tile, 1), 0)
            row = row - 96 * ((row * 683) >> 16)
            q_pos = base + row + jnp.where(row >= 48, 144, 0)
            scores = jnp.where(k_pos <= q_pos, scores, NEG)
        m_old = m_ref[sl, :]
        m_new = jnp.maximum(m_old, jnp.max(scores, axis=1, keepdims=True))
        terms = jnp.exp2(scores - jnp.concatenate([m_new] * (width // 128), axis=1))
        update = mm(terms.astype(BF), values1)
        shrink = jnp.exp2(m_old - m_new)
        a_ref[sl, :] = a_ref[sl, :] * shrink + update[:, :HEAD]
        l_ref[sl, :] = l_ref[sl, :] * shrink + update[:, HEAD:]
        m_ref[sl, :] = m_new


SET_CTX, SET_BASE, TEAM, CORE, ODD, BLOCK_CTX = 0, 2, 4, 5, 6, 7


def attend_kernel(sets, places, block0, blocks, first, last, meta, *refs):
    n, ns = len(places), len(sets)
    q_refs, refs = refs[:4], refs[4:]
    kv_refs, refs = refs[:n], refs[n:]
    if not first:
        state_in, refs = refs[: 3 * ns], refs[3 * ns :]
    if last:
        w_refs, refs = refs[:6], refs[6:]
        keep_ref, send_ref, q_scr, kv_scr, sems = refs[:5]
        m_ref, l_ref, a_ref, w_scr, w_sems, x_scr, p_scr = refs[5:]
        state = [(m_ref, l_ref, a_ref)]
    else:
        q_scr, kv_scr, sems = refs[3 * ns :]
        state = [refs[3 * i : 3 * i + 3] for i in range(ns)]
    copies = []
    for i, (kv_ref, (block, start, rows)) in enumerate(zip(kv_refs, places)):
        copy = pltpu.make_async_copy(
            kv_ref, kv_scr.at[pl.ds(block * 768 + start, rows)], sems.at[i]
        )
        copy.start()
        copies.append(copy)
    if last:
        w_copies, at = [], 0
        for i, w_ref in enumerate(w_refs):
            rows = w_ref.shape[0]
            copy = pltpu.make_async_copy(w_ref, w_scr.at[pl.ds(at, rows)], w_sems.at[i])
            copy.start()
            w_copies.append(copy)
            at += rows
    scale = np.float32(math.log2(math.e) / math.sqrt(HEAD))
    for i, s in enumerate(sets):
        for j in range(4):
            for p in range(2):
                q = q_refs[j][s, :, p * HEAD : (p + 1) * HEAD].astype(F32) * scale
                high = q.astype(BF)
                low = (q - high.astype(F32)).astype(BF)
                head = 2 * (meta[TEAM] ^ j) + p
                sl = pl.ds(pl.multiple_of(head * 96, 96), 96)
                q_scr[i, sl, :HEAD] = high
                q_scr[i, sl, HEAD:] = low
        m_ref, l_ref, a_ref = state[i]
        if first:
            m_ref[...] = jnp.full(m_ref.shape, NEG, F32)
            l_ref[...] = jnp.zeros(l_ref.shape, F32)
            a_ref[...] = jnp.zeros(a_ref.shape, F32)
        else:
            for dst, src in zip(state[i], state_in[3 * i : 3 * i + 3]):
                dst[...] = src[...]

    def step(j, carry):
        for copy, (block, _, _) in zip(copies, places):
            pl.when(j == block)(copy.wait)
        block_ctx = meta[BLOCK_CTX + block0 + j]
        sl = pl.ds(pl.multiple_of(j * 768, 768), 768)
        for i, s in enumerate(sets):
            set_ctx = meta[SET_CTX + s]

            def run(masked, i=i, s=s):
                k = kv_scr[sl, :HEAD]
                v = kv_scr[sl, HEAD:]
                keys2 = jnp.concatenate([k, k], axis=1)
                values1 = jnp.concatenate([v, jnp.ones_like(v)], axis=1)
                base = meta[SET_BASE + s]
                attend_tile(keys2, values1, base, q_scr.at[i], *state[i], masked, 256)

            pl.when(block_ctx < set_ctx)(functools.partial(run, False))
            pl.when(block_ctx == set_ctx)(functools.partial(run, True))
        return carry

    lax.fori_loop(0, blocks, step, 0)
    if last:
        k, p = meta[TEAM], meta[CORE]
        heads = [2 * k, 2 * k + 1, 2 * (k ^ 2) + p, 2 * (k ^ 1) + p]
        heads += [2 * (k ^ 3) + p, 2 * (k ^ 3) + 1 - p]
        heads += [2 * (k ^ 2) + 1 - p, 2 * (k ^ 1) + 1 - p]
        for i, head in enumerate(heads):
            sl = pl.ds(pl.multiple_of(head * 96, 96), 96)
            out = a_ref[sl, :] / l_ref[sl, :]
            x_scr[:, i * HEAD : (i + 1) * HEAD] = out.astype(BF)
        for copy in w_copies:
            copy.wait()
        for c0 in range(0, 2048, 512):
            cols = pl.ds(c0, 512)
            total = mm(x_scr[...], w_scr[:, cols])
            p_scr[0, :, cols] = total[:48]
            p_scr[1, :, cols] = total[48:]
        odd = meta[ODD]
        keep_ref[...] = p_scr[odd].astype(keep_ref.dtype)
        send_ref[...] = p_scr[1 - odd].astype(BF)


def attend(sets, meta, q, arrays, places, block0, state, weights=None, keep=None):
    ns, first, last = len(sets), state is None, weights is not None
    blocks = max(p[0] + (p[1] + p[2] + 767) // 768 for p in places)
    state_in = () if first else tuple(state)
    weights = tuple(weights or ())
    hbm = pl.BlockSpec(memory_space=pltpu.HBM)
    scratch = [
        VMEM((ns, 768, 2 * HEAD), BF),
        VMEM((blocks * 768, 2 * HEAD), BF),
        pltpu.SemaphoreType.DMA((len(arrays),)),
    ]
    if last:
        out_shape = [
            jax.ShapeDtypeStruct((48, 2048), keep),
            jax.ShapeDtypeStruct((48, 2048), BF),
        ]
        scratch = scratch + [VMEM((768, HEAD), F32)] * 3
        scratch += [VMEM((1024, 2048), BF), pltpu.SemaphoreType.DMA((6,))]
        scratch += [VMEM((96, 1024), BF), VMEM((2, 48, 2048), F32)]
    else:
        out_shape = [jax.ShapeDtypeStruct((768, HEAD), F32)] * (3 * ns)
    units = blocks * ns * 17 / 32
    return pl.pallas_call(
        functools.partial(attend_kernel, sets, tuple(places), block0, blocks, first, last),
        out_shape=out_shape,
        in_specs=[pl.BlockSpec(memory_space=pltpu.SMEM)]
        + vmem_specs(4)
        + [hbm] * len(arrays)
        + vmem_specs(len(state_in))
        + [hbm] * len(weights),
        out_specs=vmem_specs(len(out_shape)),
        scratch_shapes=scratch,
        compiler_params=params(60),
        cost_estimate=pl.CostEstimate(
            flops=int(units * 1.3e9), bytes_accessed=8 << 20, transcendentals=int(units * 600000)
        ),
        name="attend",
    )(meta, *q, *arrays, *state_in, *weights)


def iota(shape, dim):
    return lax.broadcasted_iota(jnp.int32, shape, dim)


def row_fields(row):
    device = row >> 3
    ctx = device >> 4
    expert = ((device & 15) << 3) | (ctx >> 1)
    rank = ((ctx & 1) << 1) | ((row >> 2) & 1)
    return expert, rank, row & 3


def route_kernel(ids_ref, ids_t_ref, gates_ref, send_ref, high_ref, low_ref):
    ids, ids_t, gates = ids_ref[...], ids_t_ref[...], gates_ref[...]
    expert_lane = iota((48, 128), 1)
    named = jnp.zeros((48, 128), F32)
    gate = jnp.zeros((48, 128), F32)
    expert_row = iota((128, 48), 0)
    named_t = jnp.zeros((128, 48), F32)
    for k in range(8):
        hit = ids[:, k : k + 1] == expert_lane
        named = named + jnp.where(hit, 1.0, 0.0)
        gate = gate + jnp.where(hit, gates[:, k : k + 1], 0.0)
        named_t = named_t + jnp.where(ids_t[k : k + 1, :] == expert_row, 1.0, 0.0)
    lower = jnp.where(iota((48, 48), 1) <= iota((48, 48), 0), 1.0, 0.0).astype(BF)
    upper = jnp.where(iota((48, 48), 0) <= iota((48, 48), 1), 1.0, 0.0).astype(BF)
    rank = (mm(lower, named.astype(BF)) * named).astype(BF)
    rank_t = (mm(named_t.astype(BF), upper) * named_t).astype(BF)
    high = gate.astype(BF)
    low = (gate - high.astype(F32)).astype(BF)

    expert, want, quarter = row_fields(iota((2048, 128), 0))
    pick = jnp.where(expert == iota((2048, 128), 1), 1.0, 0.0).astype(BF)
    have = mm(pick, rank_t)
    expert, want, quarter = row_fields(iota((2048, 48), 0))
    wanted = (want + 1).astype(F32)
    parts = [jnp.where((have == wanted) & (quarter == q), 1.0, 0.0) for q in range(4)]
    for q in range(4):
        send_ref[:, 48 * q : 48 * q + 48] = parts[q].astype(BF)

    expert, want, quarter = row_fields(iota((128, 2048), 1))
    pick = jnp.where(expert == iota((128, 2048), 0), 1.0, 0.0).astype(BF)
    have = mm(rank, pick)
    got_high, got_low = mm(high, pick), mm(low, pick)
    expert, want, quarter = row_fields(iota((48, 2048), 1))
    live = have == (want + 1).astype(F32)
    for q in range(4):
        here = live & (quarter == q)
        sl = pl.ds(48 * q, 48)
        high_ref[sl, :] = jnp.where(here, got_high, 0.0).astype(BF)
        low_ref[sl, :] = jnp.where(here, got_low, 0.0).astype(BF)


def route(ids, gates):
    back = jax.ShapeDtypeStruct((192, 2048), BF)
    return pl.pallas_call(
        route_kernel,
        out_shape=[jax.ShapeDtypeStruct((2048, 192), BF), back, back],
        in_specs=vmem_specs(3),
        out_specs=vmem_specs(3),
        compiler_params=params(24),
        cost_estimate=pl.CostEstimate(
            flops=400 << 20, bytes_accessed=3 << 20, transcendentals=0
        ),
        name="route",
    )(ids, ids.T, gates)


def dispatch_kernel(
    residual, own, r1, r2, r3, gain, send, mixed_ref, out_ref, stack, rows_scr, sems
):
    mixed = residual[...].astype(F32) + own[...]
    mixed = mixed + r1[...].astype(F32) + r2[...].astype(F32) + r3[...].astype(F32)
    mixed_ref[...] = mixed
    mean_square = jnp.mean(mixed * mixed, axis=-1, keepdims=True)
    normed = (mixed * lax.rsqrt(mean_square + 1e-06) * gain[...]).astype(BF)
    for q in range(4):
        stack[48 * q : 48 * q + 48, :] = normed[:, 512 * q : 512 * q + 512]
    copies = []
    for i in range(8):
        sl = pl.ds(i * 256, 256)
        rows_scr[sl, :] = mm(send[sl, :], stack[...]).astype(BF)
        copy = pltpu.make_async_copy(rows_scr.at[sl], out_ref.at[sl], sems.at[i])
        copy.start()
        copies.append(copy)
    for copy in copies:
        copy.wait()


def dispatch(residual, own, received, gain, send):
    return pl.pallas_call(
        dispatch_kernel,
        out_shape=[
            jax.ShapeDtypeStruct((48, 2048), F32),
            jax.ShapeDtypeStruct((2048, 512), BF),
        ],
        in_specs=vmem_specs(7),
        out_specs=vmem_specs(1) + [pl.BlockSpec(memory_space=pltpu.HBM)],
        scratch_shapes=[
            VMEM((192, 512), BF),
            VMEM((2048, 512), BF),
            pltpu.SemaphoreType.DMA((8,)),
        ],
        compiler_params=params(24),
        name="dispatch",
    )(residual, own, *received, gain, send)


def combine_kernel(mixed, high, low, results, out_ref):
    total = mm(high[...], results[...]) + mm(low[...], results[...])
    for q in range(4):
        cols = pl.ds(512 * q, 512)
        out_ref[:, cols] = (mixed[:, cols] + total[48 * q : 48 * q + 48]).astype(BF)


def combine(mixed, high, low, results):
    return pl.pallas_call(
        combine_kernel,
        out_shape=jax.ShapeDtypeStruct((48, 2048), BF),
        in_specs=vmem_specs(4),
        out_specs=pl.BlockSpec(memory_space=VMEM),
        compiler_params=params(24),
        name="combine",
    )(mixed, high, low, results)


def expert_kernel(
    rows_ref,
    g0,
    u0,
    d0,
    g1,
    u1,
    d1,
    out_ref,
    in_scr,
    out_scr,
    x_scr,
    hidden_scr,
    y_scr,
    gate_scr,
    up_scr,
    down_scr,
    sems,
    in_sems,
    out_sems,
):
    def block_in(b):
        sl = pl.ds(b * 256, 256)
        return pltpu.make_async_copy(rows_ref.at[sl], in_scr.at[sl], in_sems.at[b])

    def block_out(b):
        sl = pl.ds(b * 256, 256)
        return pltpu.make_async_copy(out_scr.at[sl], out_ref.at[sl], out_sems.at[b])

    for b in range(8):
        block_in(b).start()
    copies = []
    for i, (g, u, d) in enumerate(((g0, u0, d0), (g1, u1, d1))):
        part = pl.ds(384 * i, 384)
        copies.append(pltpu.make_async_copy(g, gate_scr.at[:, part], sems.at[3 * i]))
        copies.append(pltpu.make_async_copy(u, up_scr.at[:, part], sems.at[3 * i + 1]))
        copies.append(pltpu.make_async_copy(d, down_scr.at[part], sems.at[3 * i + 2]))
    for i in (0, 1, 3, 4, 2, 5):
        copies[i].start()
    to_row, from_col = iota((256, 256), 0), iota((256, 256), 1)
    sort = jnp.where(from_col == ((to_row & 63) << 2) + (to_row >> 6), 1.0, 0.0).astype(BF)
    unsort = jnp.where(to_row == ((from_col & 63) << 2) + (from_col >> 6), 1.0, 0.0).astype(BF)

    for b in range(8):
        block_in(b).wait()
        block = mm(sort, in_scr[256 * b : 256 * b + 256, :]).astype(BF)
        for q in range(4):
            x_scr[64 * b : 64 * b + 64, 512 * q : 512 * q + 512] = block[64 * q : 64 * q + 64]
    for j in range(3):
        if j < 2:
            copies[3 * j].wait()
            copies[3 * j + 1].wait()
        cols = pl.ds(256 * j, 256)

        def rise(t, carry, cols=cols):
            tokens = pl.ds(pl.multiple_of(t * 256, 256), 256)
            x = x_scr[tokens, :]
            gate = mm(x, gate_scr[:, cols])
            up = mm(x, up_scr[:, cols])
            hidden_scr[tokens, cols] = (gate / (1.0 + jnp.exp(-gate)) * up).astype(BF)
            return carry

        lax.fori_loop(0, 2, rise, 0)
    copies[2].wait()
    copies[5].wait()

    def fall(t, carry):
        tokens = pl.ds(pl.multiple_of(t * 256, 256), 256)
        for q in range(4):
            part = mm(hidden_scr[tokens, :], down_scr[:, 512 * q : 512 * q + 512])
            y_scr[q, tokens, :] = part.astype(BF)
        return carry

    lax.fori_loop(0, 2, fall, 0)
    for b in range(8):
        tokens = pl.ds(64 * b, 64)
        block = jnp.concatenate([y_scr[q, tokens, :] for q in range(4)], axis=0)
        out_scr[256 * b : 256 * b + 256, :] = mm(unsort, block).astype(BF)
        block_out(b).start()
    for b in range(8):
        block_out(b).wait()


def experts(rows, weights):
    return pl.pallas_call(
        expert_kernel,
        out_shape=jax.ShapeDtypeStruct((2048, 512), BF),
        in_specs=[pl.BlockSpec(memory_space=pltpu.HBM)] * 7,
        out_specs=pl.BlockSpec(memory_space=pltpu.HBM),
        scratch_shapes=[
            VMEM((2048, 512), BF),
            VMEM((2048, 512), BF),
            VMEM((512, 2048), BF),
            VMEM((512, 768), BF),
            VMEM((4, 512, 512), BF),
            VMEM((2048, 768), BF),
            VMEM((2048, 768), BF),
            VMEM((768, 2048), BF),
            pltpu.SemaphoreType.DMA((6,)),
            pltpu.SemaphoreType.DMA((8,)),
            pltpu.SemaphoreType.DMA((8,)),
        ],
        compiler_params=params(60),
        name="experts",
    )(rows, *weights)


def along_ctx(x, source_of):
    return lax.ppermute(x, "ctx", [(source_of(c), c) for c in range(16)])


def along_exp(x, flip):
    return lax.ppermute(x, "exp", [(e ^ flip, e) for e in range(16)])


def along_both(x, mirror, flip):
    pairs = [
        (c * 16 + e, ((15 - c) if mirror else c) * 16 + (e ^ flip))
        for c in range(16)
        for e in range(16)
    ]
    return lax.ppermute(x, ("ctx", "exp"), pairs)


def local(
    queries,
    keys,
    values,
    out_weight,
    residual,
    norm_gain,
    route_ids,
    route_gates,
    w_gate,
    w_up,
    w_down,
):
    c = lax.axis_index("ctx")
    e = lax.axis_index("exp")
    core, g, k = c % 2, e // 4, e % 4
    pair = g // 2

    kv_head = e // 8
    own = jnp.concatenate(
        [
            lax.dynamic_slice_in_dim(keys, kv_head * HEAD, HEAD, 1),
            lax.dynamic_slice_in_dim(values, kv_head * HEAD, HEAD, 1),
        ],
        axis=1,
    )

    def swap(x):
        return along_ctx(x, lambda i: i ^ 1)

    def from_y(x):
        return along_ctx(x, lambda i: i ^ 2)

    def from_x(x, step):
        return along_ctx(x, lambda i: (i + 4 * step) % 16)

    n1, n2, n3 = from_x(own, 1), from_x(own, -1), from_y(own)
    x, y = c // 4, (c // 2) % 2

    def ctx_of(dx, dy, dp):
        return ((x + dx) % 4) * 4 + (y ^ dy) * 2 + (core ^ dp)

    grouped = queries.reshape(2, 2, 4, 48, 256)
    q_own = lax.dynamic_index_in_dim(grouped, pair, 0, False)
    q_mirror = along_ctx(lax.dynamic_index_in_dim(grouped, 1 - pair, 0, False), lambda i: 15 - i)
    w_part = lax.dynamic_slice_in_dim(out_weight, core * HEAD, HEAD, 0)

    def from_team(flip_ctx, flip_exp):
        pairs = [
            (i * 16 + j, (i ^ flip_ctx) * 16 + (j ^ flip_exp))
            for i in range(16)
            for j in range(16)
        ]
        return lax.ppermute(w_part, ("ctx", "exp"), pairs)

    wz = from_team(0, 2)

    order = [(0, 0, 0), (0, 0, 1), (1, 0, 0), (3, 0, 0), (0, 1, 0)]
    order += [(1, 0, 1), (3, 0, 1), (0, 1, 1), (2, 0, 0), (3, 1, 0), (1, 1, 0)]
    order += [(2, 0, 1), (3, 1, 1), (1, 1, 1), (2, 1, 0), (2, 1, 1)]
    meta = jnp.stack(
        [15 - c, c, (8 * (1 - pair) + k) * 48, (8 * pair + k) * 48, k, core, g % 2]
        + [ctx_of(*place) for place in order]
    ).astype(jnp.int32)

    n1, n2, n3, q_mirror, wz = lax.optimization_barrier((n1, n2, n3, q_mirror, wz))
    q = []
    for j in range(4):
        piece = jnp.stack(
            [
                lax.dynamic_index_in_dim(half, k ^ j, 1, False).reshape(96, 256)
                for half in (q_mirror, q_own)
            ]
        )
        q.append(along_exp(piece, j) if j else piece)
    own_s = swap(own)
    n4 = from_x(n1, 1)
    q, own_s = lax.optimization_barrier((q, own_s))
    n5, n6 = from_x(n3, -1), from_y(n1)
    s123 = swap(jnp.concatenate([n1, n2, n3], axis=0))
    wy = from_team(2, 1)
    near = [own, own_s, n1, n2, n3]
    state = attend((0, 1), meta, q, near, [(i, 0, 768) for i in range(5)], 0, None)

    state, n4, n5, n6, s123, wy = lax.optimization_barrier((state, n4, n5, n6, s123, wy))
    n7a, n7b = from_y(n4[:384]), from_x(n6[384:], 1)
    wzy = from_team(2, 3)
    s456 = swap(jnp.concatenate([n4, n5, n6], axis=0))
    woa = swap(jnp.concatenate([wz, wy], axis=0))
    middle = [s123, n4, n5, n6]
    at_middle = [(0, 0, 2304), (3, 0, 768), (4, 0, 768), (5, 0, 768)]
    mirror = attend((0,), meta, q, middle, at_middle, 5, state[:3])

    mirror, n7a, n7b, s456, wzy, woa = lax.optimization_barrier(
        (mirror, n7a, n7b, s456, wzy, woa)
    )
    s7 = swap(jnp.concatenate([n7a, n7b], axis=0))
    wob = swap(wzy)
    far = [s456, n7a, n7b, s7]
    at_far = [(0, 0, 2304), (3, 0, 384), (3, 384, 384), (4, 0, 768)]
    weights = [out_weight, wz, wy, wzy, wob, woa]
    t2, t3 = attend((0,), meta, q, far, at_far, 11, mirror, weights, BF)
    at_far = [(at[0] + 6,) + at[1:] for at in at_far]
    t2, t3, state = lax.optimization_barrier((t2, t3, state))
    received = [along_both(t2, True, 8), along_both(t3, True, 12)]
    mine, t1 = attend(
        (1,), meta, q, middle + far, at_middle + at_far, 5, state[3:], weights, F32
    )
    t1, received = lax.optimization_barrier((t1, received))
    received.append(along_both(t1, False, 4))

    send, back_high, back_low = route(route_ids, route_gates)
    mixed, rows = dispatch(residual, mine, received, norm_gain[None, :], send)

    own_w = [w_gate[0, 0], w_up[0, 0], w_down[0, 0]]
    other_w = [swap(w) for w in own_w]

    def exchange(v):
        return lax.all_to_all(
            v.reshape(256, 8, 512), ("ctx", "exp"), split_axis=0, concat_axis=0, tiled=True
        ).reshape(2048, 512)

    results = exchange(experts(exchange(rows), own_w + other_w))
    return combine(mixed, back_high, back_low, results)


def solution(mesh):
    placed = (
        P("ctx", "exp"),
        P("ctx", None),
        P("ctx", None),
        P("exp", None),
        P(("ctx", "exp"), None),
        P(),
        P(("ctx", "exp"), None),
        P(("ctx", "exp"), None),
        P("ctx", "exp", None, None),
        P("ctx", "exp", None, None),
        P("ctx", "exp", None, None),
    )
    return jax.shard_map(
        local, mesh=mesh, in_specs=placed, out_specs=P(("ctx", "exp"), None), check_vma=False
    )
```

```python
import functools
import math

import jax
import jax.numpy as jnp
import numpy as np
from jax import lax
from jax.experimental import pallas as pl
from jax.experimental.pallas import tpu as pltpu
from jax.sharding import PartitionSpec as P

HEAD = 128
NEG = -1e30
BF = jnp.bfloat16
F32 = jnp.float32
VMEM = pltpu.VMEM
MIB = 1 << 20


def params(mib):
    return pltpu.CompilerParams(vmem_limit_bytes=mib * MIB)


def vmem_specs(count):
    return [pl.BlockSpec(memory_space=VMEM)] * count


def mm(a, b):
    return jnp.dot(a, b, preferred_element_type=F32)


SET_CTX, BASE, HALF, PLACE, TEAM, CORE, BLOCK_CTX = 0, 2, 6, 10, 12, 13, 14


def iota(shape, dim):
    return lax.broadcasted_iota(jnp.int32, shape, dim)


def attend_rows(tiles, keys2, values1, bases):
    width = keys2.shape[0]
    scores = []
    for i, tile in enumerate(tiles):
        part = lax.dot_general(
            tile[0][...], keys2, (((1,), (1,)), ((), ())), preferred_element_type=F32
        )
        if bases is not None:
            row = iota((384, 1), 0)
            q_pos = bases[i] + row - 48 * ((row * 1366) >> 16)
            part = jnp.where(iota((384, width), 1) <= q_pos, part, NEG)
        scores.append(part)
    terms, maxima = [], []
    for part, (_, m_ref, _, _) in zip(scores, tiles):
        m_old = m_ref[...]
        m_new = jnp.maximum(m_old, jnp.max(part, axis=1, keepdims=True))
        wide = jnp.concatenate([m_new] * (width // 128), axis=1)
        terms.append(jnp.exp2(part - wide).astype(BF))
        maxima.append((m_old, m_new))
    for part, (m_old, m_new), (_, m_ref, l_ref, a_ref) in zip(terms, maxima, tiles):
        update = mm(part, values1)
        shrink = jnp.exp2(m_old - m_new)
        a_ref[...] = a_ref[...] * shrink + update[:, :HEAD]
        l_ref[...] = l_ref[...] * shrink + update[:, HEAD:]
        m_ref[...] = m_new


def attend_kernel(parts, places, block0, blocks, first, last, meta, *refs):
    n, ns = len(places), len(parts)
    q_ref, refs = refs[0], refs[1:]
    kv_refs, refs = refs[:n], refs[n:]
    if not first:
        state_in, refs = refs[: 3 * ns], refs[3 * ns :]
    if last:
        o_ref, q_scr, kv_scr, sems, m_scr, l_scr, a_scr = refs
        state = [(m_scr.at[i], l_scr.at[i], a_scr.at[i]) for i in range(ns)]
    else:
        q_scr, kv_scr, sems = refs[3 * ns :]
        state = [tuple(refs[3 * i : 3 * i + 3]) for i in range(ns)]
    copies = []
    for i, (kv_ref, (block, start, rows)) in enumerate(zip(kv_refs, places)):
        copy = pltpu.make_async_copy(
            kv_ref, kv_scr.at[pl.ds(block * 768 + start, rows)], sems.at[i]
        )
        copy.start()
        copies.append(copy)
    scale = np.float32(math.log2(math.e) / math.sqrt(HEAD))
    for i, part in enumerate(parts):
        half, place = meta[HALF + part], meta[PLACE + part % 2]
        for k in range(4):
            for p in range(2):
                q = q_ref[place, k, half, :, p * HEAD : (p + 1) * HEAD].astype(F32) * scale
                high = q.astype(BF)
                low = (q - high.astype(F32)).astype(BF)
                sl = pl.ds((2 * k + p) * 48, 48)
                q_scr[i, sl, :HEAD] = high
                q_scr[i, sl, HEAD:] = low
        m_ref, l_ref, a_ref = state[i]
        if first:
            m_ref[...] = jnp.full(m_ref.shape, NEG, F32)
            l_ref[...] = jnp.zeros(l_ref.shape, F32)
            a_ref[...] = jnp.zeros(a_ref.shape, F32)
        else:
            for dst, src in zip(state[i], state_in[3 * i : 3 * i + 3]):
                dst[...] = src[...]
    mirror = [i for i in range(ns) if parts[i] % 2 == 0]
    own = [i for i in range(ns) if parts[i] % 2 == 1]
    mirror_ctx, own_ctx = meta[SET_CTX], meta[SET_CTX + 1]

    def step(j, carry):
        for copy, (block, _, _) in zip(copies, places):
            pl.when(j == block)(copy.wait)
        block_ctx = meta[BLOCK_CTX + block0 + j]
        sl = pl.ds(pl.multiple_of(j * 768, 768), 768)

        def run(chosen, masked):
            k = kv_scr[sl, :HEAD]
            v = kv_scr[sl, HEAD:]
            keys2 = jnp.concatenate([k, k], axis=1)
            values1 = jnp.concatenate([v, jnp.ones_like(v)], axis=1)
            tiles = [(q_scr.at[i],) + state[i] for i in chosen]
            bases = [meta[BASE + parts[i]] for i in chosen] if masked else None
            attend_rows(tiles, keys2, values1, bases)

        to_mirror, to_own = block_ctx < mirror_ctx, block_ctx < own_ctx
        pl.when(to_mirror & to_own)(lambda: run(mirror + own, False))
        pl.when(to_mirror & jnp.logical_not(to_own))(lambda: run(mirror, False))
        pl.when(to_own & jnp.logical_not(to_mirror))(lambda: run(own, False))
        pl.when(block_ctx == mirror_ctx)(lambda: run(mirror, True))
        pl.when(block_ctx == own_ctx)(lambda: run(own, True))
        return carry

    lax.fori_loop(0, blocks, step, 0)
    if last:
        o_ref[...] = (a_scr[...] / l_scr[...]).astype(BF).reshape(o_ref.shape)


def attend(parts, meta, q, arrays, places, block0, state):
    ns, first, last = len(parts), state is None, state is not None
    blocks = max(p[0] + (p[1] + p[2] + 767) // 768 for p in places)
    state_in = () if first else tuple(state)
    scratch = [
        VMEM((ns, 384, 2 * HEAD), BF),
        VMEM((blocks * 768, 2 * HEAD), BF),
        pltpu.SemaphoreType.DMA((len(arrays),)),
    ]
    if last:
        out_shape = [jax.ShapeDtypeStruct((ns, 8, 48, HEAD), BF)]
        scratch = scratch + [VMEM((ns, 384, HEAD), F32)] * 3
    else:
        out_shape = [jax.ShapeDtypeStruct((384, HEAD), F32)] * (3 * ns)
    units = blocks * ns * 17 / 64
    return pl.pallas_call(
        functools.partial(attend_kernel, parts, tuple(places), block0, blocks, first, last),
        out_shape=out_shape,
        in_specs=[pl.BlockSpec(memory_space=pltpu.SMEM)]
        + vmem_specs(1)
        + [pl.BlockSpec(memory_space=pl.ANY)] * len(arrays)
        + vmem_specs(len(state_in)),
        out_specs=vmem_specs(len(out_shape)),
        scratch_shapes=scratch,
        compiler_params=params(32),
        cost_estimate=pl.CostEstimate(
            flops=int(units * 1.3e9), bytes_accessed=8 << 20, transcendentals=int(units * 600000)
        ),
        name="attend",
    )(meta, q, *arrays, *state_in)


def project_kernel(
    meta, att_ref, w0, w1, w2, w3, w4, o0, o1, o2, o3, w_scr, x_scr, sems
):
    copies, at = [], 0
    for j, w_ref in enumerate((w0, w1, w2, w3, w4)):
        rows = w_ref.shape[0]
        copies.append(pltpu.make_async_copy(w_ref, w_scr.at[pl.ds(at, rows)], sems.at[j]))
        copies[j].start()
        at += rows
    k, p = meta[TEAM], meta[CORE]
    heads = [2 * k, 2 * k + 1]
    heads += [2 * (k ^ j) + p for j in (1, 2, 3)]
    heads += [2 * (k ^ j) + 1 - p for j in (1, 2, 3)]
    for i in range(4):
        for j, head in enumerate(heads):
            x_scr[48 * i : 48 * i + 48, j * HEAD : (j + 1) * HEAD] = att_ref[i, head]
    for copy in copies:
        copy.wait()
    for c0 in range(0, 2048, 512):
        cols = pl.ds(c0, 512)
        total = mm(x_scr[...], w_scr[:, cols])
        for i, o_ref in enumerate((o0, o1, o2, o3)):
            o_ref[:, cols] = total[48 * i : 48 * i + 48].astype(o_ref.dtype)


def project(meta, att, weights):
    sent = jax.ShapeDtypeStruct((48, 2048), BF)
    return pl.pallas_call(
        project_kernel,
        out_shape=[sent, sent, sent, jax.ShapeDtypeStruct((48, 2048), F32)],
        in_specs=[pl.BlockSpec(memory_space=pltpu.SMEM)]
        + vmem_specs(1)
        + [pl.BlockSpec(memory_space=pl.ANY)] * 5,
        out_specs=vmem_specs(4),
        scratch_shapes=[
            VMEM((1024, 2048), BF),
            VMEM((192, 1024), BF),
            pltpu.SemaphoreType.DMA((5,)),
        ],
        compiler_params=params(24),
        name="project",
    )(meta, att, *weights)


def row_fields(row):
    device = row >> 3
    ctx = device >> 4
    expert = ((device & 15) << 3) | (ctx >> 1)
    rank = ((ctx & 1) << 1) | ((row >> 2) & 1)
    return expert, rank, row & 3


def route_kernel(ids_ref, ids_t_ref, gates_ref, send_ref, high_ref, low_ref):
    ids, ids_t, gates = ids_ref[...], ids_t_ref[...], gates_ref[...]
    expert_lane = iota((48, 128), 1)
    named = jnp.zeros((48, 128), F32)
    gate = jnp.zeros((48, 128), F32)
    expert_row = iota((128, 48), 0)
    named_t = jnp.zeros((128, 48), F32)
    for k in range(8):
        hit = ids[:, k : k + 1] == expert_lane
        named = named + jnp.where(hit, 1.0, 0.0)
        gate = gate + jnp.where(hit, gates[:, k : k + 1], 0.0)
        named_t = named_t + jnp.where(ids_t[k : k + 1, :] == expert_row, 1.0, 0.0)
    lower = jnp.where(iota((48, 48), 1) <= iota((48, 48), 0), 1.0, 0.0).astype(BF)
    upper = jnp.where(iota((48, 48), 0) <= iota((48, 48), 1), 1.0, 0.0).astype(BF)
    rank = (mm(lower, named.astype(BF)) * named).astype(BF)
    rank_t = (mm(named_t.astype(BF), upper) * named_t).astype(BF)
    high = gate.astype(BF)
    low = (gate - high.astype(F32)).astype(BF)

    expert, want, quarter = row_fields(iota((2048, 128), 0))
    pick = jnp.where(expert == iota((2048, 128), 1), 1.0, 0.0).astype(BF)
    have = mm(pick, rank_t)
    expert, want, quarter = row_fields(iota((2048, 48), 0))
    wanted = (want + 1).astype(F32)
    parts = [jnp.where((have == wanted) & (quarter == q), 1.0, 0.0) for q in range(4)]
    for q in range(4):
        send_ref[:, 48 * q : 48 * q + 48] = parts[q].astype(BF)

    expert, want, quarter = row_fields(iota((128, 2048), 1))
    pick = jnp.where(expert == iota((128, 2048), 0), 1.0, 0.0).astype(BF)
    have = mm(rank, pick)
    got_high, got_low = mm(high, pick), mm(low, pick)
    expert, want, quarter = row_fields(iota((48, 2048), 1))
    live = have == (want + 1).astype(F32)
    for q in range(4):
        here = live & (quarter == q)
        sl = pl.ds(48 * q, 48)
        high_ref[sl, :] = jnp.where(here, got_high, 0.0).astype(BF)
        low_ref[sl, :] = jnp.where(here, got_low, 0.0).astype(BF)


def route(ids, gates):
    back = jax.ShapeDtypeStruct((192, 2048), BF)
    return pl.pallas_call(
        route_kernel,
        out_shape=[jax.ShapeDtypeStruct((2048, 192), BF), back, back],
        in_specs=vmem_specs(3),
        out_specs=vmem_specs(3),
        compiler_params=params(24),
        cost_estimate=pl.CostEstimate(
            flops=400 << 20, bytes_accessed=3 << 20, transcendentals=0
        ),
        name="route",
    )(ids, ids.T, gates)


def dispatch_kernel(
    residual, own, r1, r2, r3, gain, send, mixed_ref, out_ref, stack, rows_scr, sems
):
    mixed = residual[...].astype(F32) + own[...]
    mixed = mixed + r1[...].astype(F32) + r2[...].astype(F32) + r3[...].astype(F32)
    mixed_ref[...] = mixed
    mean_square = jnp.mean(mixed * mixed, axis=-1, keepdims=True)
    normed = (mixed * lax.rsqrt(mean_square + 1e-06) * gain[...]).astype(BF)
    for q in range(4):
        stack[48 * q : 48 * q + 48, :] = normed[:, 512 * q : 512 * q + 512]
    copies = []
    for i in range(8):
        sl = pl.ds(i * 256, 256)
        rows_scr[sl, :] = mm(send[sl, :], stack[...]).astype(BF)
        copy = pltpu.make_async_copy(rows_scr.at[sl], out_ref.at[sl], sems.at[i])
        copy.start()
        copies.append(copy)
    for copy in copies:
        copy.wait()


def dispatch(residual, own, received, gain, send):
    return pl.pallas_call(
        dispatch_kernel,
        out_shape=[
            jax.ShapeDtypeStruct((48, 2048), F32),
            jax.ShapeDtypeStruct((2048, 512), BF),
        ],
        in_specs=vmem_specs(7),
        out_specs=vmem_specs(1) + [pl.BlockSpec(memory_space=pltpu.HBM)],
        scratch_shapes=[
            VMEM((192, 512), BF),
            VMEM((2048, 512), BF),
            pltpu.SemaphoreType.DMA((8,)),
        ],
        compiler_params=params(24),
        name="dispatch",
    )(residual, own, *received, gain, send)


def combine_kernel(mixed, high, low, results, out_ref):
    total = mm(high[...], results[...]) + mm(low[...], results[...])
    for q in range(4):
        cols = pl.ds(512 * q, 512)
        out_ref[:, cols] = (mixed[:, cols] + total[48 * q : 48 * q + 48]).astype(BF)


def combine(mixed, high, low, results):
    return pl.pallas_call(
        combine_kernel,
        out_shape=jax.ShapeDtypeStruct((48, 2048), BF),
        in_specs=vmem_specs(4),
        out_specs=pl.BlockSpec(memory_space=VMEM),
        compiler_params=params(24),
        name="combine",
    )(mixed, high, low, results)


def expert_kernel(
    rows_ref,
    g0,
    u0,
    d0,
    g1,
    u1,
    d1,
    out_ref,
    in_scr,
    out_scr,
    x_scr,
    hidden_scr,
    y_scr,
    gate_scr,
    up_scr,
    down_scr,
    sems,
    in_sems,
    out_sems,
):
    def block_in(b):
        sl = pl.ds(b * 256, 256)
        return pltpu.make_async_copy(rows_ref.at[sl], in_scr.at[sl], in_sems.at[b])

    def block_out(b):
        sl = pl.ds(b * 256, 256)
        return pltpu.make_async_copy(out_scr.at[sl], out_ref.at[sl], out_sems.at[b])

    for b in range(8):
        block_in(b).start()
    copies = []
    for i, (g, u, d) in enumerate(((g0, u0, d0), (g1, u1, d1))):
        part = pl.ds(384 * i, 384)
        copies.append(pltpu.make_async_copy(g, gate_scr.at[:, part], sems.at[3 * i]))
        copies.append(pltpu.make_async_copy(u, up_scr.at[:, part], sems.at[3 * i + 1]))
        copies.append(pltpu.make_async_copy(d, down_scr.at[part], sems.at[3 * i + 2]))
    for i in (0, 1, 3, 4, 2, 5):
        copies[i].start()
    to_row, from_col = iota((256, 256), 0), iota((256, 256), 1)
    sort = jnp.where(from_col == ((to_row & 63) << 2) + (to_row >> 6), 1.0, 0.0).astype(BF)
    unsort = jnp.where(to_row == ((from_col & 63) << 2) + (from_col >> 6), 1.0, 0.0).astype(BF)

    for b in range(8):
        block_in(b).wait()
        block = mm(sort, in_scr[256 * b : 256 * b + 256, :]).astype(BF)
        for q in range(4):
            x_scr[64 * b : 64 * b + 64, 512 * q : 512 * q + 512] = block[64 * q : 64 * q + 64]
    for j in range(3):
        if j < 2:
            copies[3 * j].wait()
            copies[3 * j + 1].wait()
        cols = pl.ds(256 * j, 256)

        def rise(t, carry, cols=cols):
            tokens = pl.ds(pl.multiple_of(t * 256, 256), 256)
            x = x_scr[tokens, :]
            gate = mm(x, gate_scr[:, cols])
            up = mm(x, up_scr[:, cols])
            hidden_scr[tokens, cols] = (gate / (1.0 + jnp.exp(-gate)) * up).astype(BF)
            return carry

        lax.fori_loop(0, 2, rise, 0)
    copies[2].wait()
    copies[5].wait()

    def fall(t, carry):
        tokens = pl.ds(pl.multiple_of(t * 256, 256), 256)
        for q in range(4):
            part = mm(hidden_scr[tokens, :], down_scr[:, 512 * q : 512 * q + 512])
            y_scr[q, tokens, :] = part.astype(BF)
        return carry

    lax.fori_loop(0, 2, fall, 0)
    for b in range(8):
        tokens = pl.ds(64 * b, 64)
        block = jnp.concatenate([y_scr[q, tokens, :] for q in range(4)], axis=0)
        out_scr[256 * b : 256 * b + 256, :] = mm(unsort, block).astype(BF)
        block_out(b).start()
    for b in range(8):
        block_out(b).wait()


def experts(rows, weights):
    return pl.pallas_call(
        expert_kernel,
        out_shape=jax.ShapeDtypeStruct((2048, 512), BF),
        in_specs=[pl.BlockSpec(memory_space=pltpu.HBM)] * 7,
        out_specs=pl.BlockSpec(memory_space=pltpu.HBM),
        scratch_shapes=[
            VMEM((2048, 512), BF),
            VMEM((2048, 512), BF),
            VMEM((512, 2048), BF),
            VMEM((512, 768), BF),
            VMEM((4, 512, 512), BF),
            VMEM((2048, 768), BF),
            VMEM((2048, 768), BF),
            VMEM((768, 2048), BF),
            pltpu.SemaphoreType.DMA((6,)),
            pltpu.SemaphoreType.DMA((8,)),
            pltpu.SemaphoreType.DMA((8,)),
        ],
        compiler_params=params(60),
        name="experts",
    )(rows, *weights)


def along_ctx(x, source_of):
    return lax.ppermute(x, "ctx", [(source_of(c), c) for c in range(16)])


def along_exp(x, flip):
    return lax.ppermute(x, "exp", [(e ^ flip, e) for e in range(16)])


def along_both(x, mirror, flip):
    pairs = [
        (c * 16 + e, ((15 - c) if mirror else c) * 16 + (e ^ flip))
        for c in range(16)
        for e in range(16)
    ]
    return lax.ppermute(x, ("ctx", "exp"), pairs)


def local(
    queries,
    keys,
    values,
    out_weight,
    residual,
    norm_gain,
    route_ids,
    route_gates,
    w_gate,
    w_up,
    w_down,
):
    c = lax.axis_index("ctx")
    e = lax.axis_index("exp")
    core, g, k = c % 2, e // 4, e % 4
    pair = g // 2

    kv_head = e // 8
    own = jnp.concatenate(
        [
            lax.dynamic_slice_in_dim(keys, kv_head * HEAD, HEAD, 1),
            lax.dynamic_slice_in_dim(values, kv_head * HEAD, HEAD, 1),
        ],
        axis=1,
    )

    def swap(x):
        return along_ctx(x, lambda i: i ^ 1)

    def from_y(x):
        return along_ctx(x, lambda i: i ^ 2)

    def from_x(x, step):
        return along_ctx(x, lambda i: (i + 4 * step) % 16)

    n1, n2, n3 = from_x(own, 1), from_x(own, -1), from_y(own)
    x, y = c // 4, (c // 2) % 2

    def ctx_of(dx, dy, dp):
        return ((x + dx) % 4) * 4 + (y ^ dy) * 2 + (core ^ dp)

    high_ctx = (c >= 8).astype(jnp.int32)
    grouped = queries.reshape(2, 2, 4, 48, 256).transpose(0, 2, 1, 3, 4)
    outgoing = jnp.where((pair + high_ctx) % 2 == 0, grouped, grouped[::-1])
    teams = [
        [cc * 16 + gg * 4 + kk for cc in (low, 15 - low) for kk in range(4)]
        for low in range(8)
        for gg in range(4)
    ]
    q = lax.all_to_all(
        outgoing.reshape(8, 2, 48, 256),
        ("ctx", "exp"),
        split_axis=0,
        concat_axis=0,
        tiled=True,
        axis_index_groups=teams,
    ).reshape(2, 4, 2, 48, 256)
    w_part = lax.dynamic_slice_in_dim(out_weight, core * HEAD, HEAD, 0)

    w1 = lax.ppermute(
        w_part,
        ("ctx", "exp"),
        [(i * 16 + j, (i ^ 2) * 16 + (j ^ 1)) for i in range(16) for j in range(16)],
    )

    near = [(0, 0), (1, 0), (3, 0), (0, 1)]
    far = [(2, 0), (3, 1), (1, 1), (2, 1)]
    order = [(dx, dy, dp) for half in (near, far) for dp in (0, 1) for dx, dy in half]
    odd = g % 2
    halves = [odd, 1 - odd, 1 - odd, odd]
    pairs = [1 - pair, pair, 1 - pair, pair]
    bases = [((2 * pp + half) * 4 + k) * 48 for pp, half in zip(pairs, halves)]
    meta = jnp.stack(
        [15 - c, c] + bases + halves + [1 - high_ctx, high_ctx, k, core] + [ctx_of(*place) for place in order]
    ).astype(jnp.int32)

    n1, n2, n3, q, w1, meta = lax.optimization_barrier((n1, n2, n3, q, w1, meta))
    s_near = swap(jnp.concatenate([own, n1, n2, n3], axis=0))
    w23 = along_exp(jnp.concatenate([w_part, w1], axis=0), 2)
    n4, n5, n6 = from_x(n1, 1), from_x(n3, -1), from_y(n1)
    n7 = along_ctx(own, lambda i: (i ^ 2) ^ 8)
    parts = (0, 1, 2, 3)
    places = [(i, 0, 768) for i in range(4)] + [(4, 0, 3072)]
    state = attend(parts, meta, q, [own, n1, n2, n3, s_near], places, 0, None)

    state, n4, n5, n6, n7, w23 = lax.optimization_barrier((state, n4, n5, n6, n7, w23))
    s_far = swap(jnp.concatenate([n4, n5, n6, n7], axis=0))
    w1_other, w23_other = swap(w1), swap(w23)
    (attended,) = attend(parts, meta, q, [n4, n5, n6, n7, s_far], places, 8, state)
    weights = [out_weight, w1, w23, w1_other, w23_other]
    t2, t1, t3, mine = project(meta, attended, weights)
    received = [along_both(t2, True, 8), along_both(t3, True, 12), along_both(t1, False, 4)]

    send, back_high, back_low = route(route_ids, route_gates)
    mixed, rows = dispatch(residual, mine, received, norm_gain[None, :], send)

    own_w = [w_gate[0, 0], w_up[0, 0], w_down[0, 0]]
    other_w = [swap(w) for w in own_w]

    def exchange(v):
        return lax.all_to_all(
            v.reshape(256, 8, 512), ("ctx", "exp"), split_axis=0, concat_axis=0, tiled=True
        ).reshape(2048, 512)

    results = exchange(experts(exchange(rows), own_w + other_w))
    return combine(mixed, back_high, back_low, results)


def solution(mesh):
    placed = (
        P("ctx", "exp"),
        P("ctx", None),
        P("ctx", None),
        P("exp", None),
        P(("ctx", "exp"), None),
        P(),
        P(("ctx", "exp"), None),
        P(("ctx", "exp"), None),
        P("ctx", "exp", None, None),
        P("ctx", "exp", None, None),
        P("ctx", "exp", None, None),
    )
    return jax.shard_map(
        local, mesh=mesh, in_specs=placed, out_specs=P(("ctx", "exp"), None), check_vma=False
    )
```

```python
import functools
import math

import jax
import jax.numpy as jnp
import numpy as np
from jax import lax
from jax.experimental import pallas as pl
from jax.experimental.pallas import tpu as pltpu
from jax.sharding import PartitionSpec as P

HEAD = 128
NEG = -1e30
BF = jnp.bfloat16
F32 = jnp.float32
VMEM = pltpu.VMEM
MIB = 1 << 20


def params(mib):
    return pltpu.CompilerParams(vmem_limit_bytes=mib * MIB)


def vmem_specs(count):
    return [pl.BlockSpec(memory_space=VMEM)] * count


def mm(a, b):
    return jnp.dot(a, b, preferred_element_type=F32)


SET_CTX, BASE, HALF, PLACE, TEAM, CORE, BLOCK_CTX = 0, 2, 6, 10, 12, 13, 14


def iota(shape, dim):
    return lax.broadcasted_iota(jnp.int32, shape, dim)


def attend_rows(tiles, keys2, values1, bases):
    width = keys2.shape[0]
    scores = []
    for i, tile in enumerate(tiles):
        part = lax.dot_general(
            tile[0][...], keys2, (((1,), (1,)), ((), ())), preferred_element_type=F32
        )
        if bases is not None:
            row = iota((384, 1), 0)
            q_pos = bases[i] + row - 48 * ((row * 1366) >> 16)
            part = jnp.where(iota((384, width), 1) <= q_pos, part, NEG)
        scores.append(part)
    terms, maxima = [], []
    for part, (_, m_ref, _, _) in zip(scores, tiles):
        m_old = m_ref[...]
        m_new = jnp.maximum(m_old, jnp.max(part, axis=1, keepdims=True))
        wide = jnp.concatenate([m_new] * (width // 128), axis=1)
        terms.append(jnp.exp2(part - wide).astype(BF))
        maxima.append((m_old, m_new))
    for part, (m_old, m_new), (_, m_ref, l_ref, a_ref) in zip(terms, maxima, tiles):
        update = mm(part, values1)
        shrink = jnp.exp2(m_old - m_new)
        a_ref[...] = a_ref[...] * shrink + update[:, :HEAD]
        l_ref[...] = l_ref[...] * shrink + update[:, HEAD:]
        m_ref[...] = m_new


def attend_kernel(parts, places, block0, blocks, first, last, meta, *refs):
    n, ns = len(places), len(parts)
    q_ref, refs = refs[0], refs[1:]
    kv_refs, refs = refs[:n], refs[n:]
    if not first:
        state_in, refs = refs[: 3 * ns], refs[3 * ns :]
    if last:
        o_ref, q_scr, kv_scr, sems, m_scr, l_scr, a_scr = refs
        state = [(m_scr.at[i], l_scr.at[i], a_scr.at[i]) for i in range(ns)]
    else:
        q_scr, kv_scr, sems = refs[3 * ns :]
        state = [tuple(refs[3 * i : 3 * i + 3]) for i in range(ns)]
    copies = []
    for i, (kv_ref, (block, start, rows)) in enumerate(zip(kv_refs, places)):
        copy = pltpu.make_async_copy(
            kv_ref, kv_scr.at[pl.ds(block * 768 + start, rows)], sems.at[i]
        )
        copy.start()
        copies.append(copy)
    scale = np.float32(math.log2(math.e) / math.sqrt(HEAD))
    for i, part in enumerate(parts):
        half, place = meta[HALF + part], meta[PLACE + part % 2]
        for k in range(4):
            for p in range(2):
                q = q_ref[place, k, half, :, p * HEAD : (p + 1) * HEAD].astype(F32) * scale
                high = q.astype(BF)
                low = (q - high.astype(F32)).astype(BF)
                sl = pl.ds((2 * k + p) * 48, 48)
                q_scr[i, sl, :HEAD] = high
                q_scr[i, sl, HEAD:] = low
        m_ref, l_ref, a_ref = state[i]
        if first:
            m_ref[...] = jnp.full(m_ref.shape, NEG, F32)
            l_ref[...] = jnp.zeros(l_ref.shape, F32)
            a_ref[...] = jnp.zeros(a_ref.shape, F32)
        else:
            for dst, src in zip(state[i], state_in[3 * i : 3 * i + 3]):
                dst[...] = src[...]
    mirror = [i for i in range(ns) if parts[i] % 2 == 0]
    own = [i for i in range(ns) if parts[i] % 2 == 1]
    mirror_ctx, own_ctx = meta[SET_CTX], meta[SET_CTX + 1]

    def step(j, carry):
        for copy, (block, _, _) in zip(copies, places):
            pl.when(j == block)(copy.wait)
        block_ctx = meta[BLOCK_CTX + block0 + j]
        sl = pl.ds(pl.multiple_of(j * 768, 768), 768)

        def run(chosen, masked):
            k = kv_scr[sl, :HEAD]
            v = kv_scr[sl, HEAD:]
            keys2 = jnp.concatenate([k, k], axis=1)
            values1 = jnp.concatenate([v, jnp.ones_like(v)], axis=1)
            tiles = [(q_scr.at[i],) + state[i] for i in chosen]
            bases = [meta[BASE + parts[i]] for i in chosen] if masked else None
            attend_rows(tiles, keys2, values1, bases)

        to_mirror, to_own = block_ctx < mirror_ctx, block_ctx < own_ctx
        pl.when(to_mirror & to_own)(lambda: run(mirror + own, False))
        pl.when(to_mirror & jnp.logical_not(to_own))(lambda: run(mirror, False))
        pl.when(to_own & jnp.logical_not(to_mirror))(lambda: run(own, False))
        pl.when(block_ctx == mirror_ctx)(lambda: run(mirror, True))
        pl.when(block_ctx == own_ctx)(lambda: run(own, True))
        return carry

    lax.fori_loop(0, blocks, step, 0)
    if last:
        o_ref[...] = (a_scr[...] / l_scr[...]).astype(BF).reshape(o_ref.shape)


def attend(parts, meta, q, arrays, places, block0, state):
    ns, first, last = len(parts), state is None, state is not None
    blocks = max(p[0] + (p[1] + p[2] + 767) // 768 for p in places)
    state_in = () if first else tuple(state)
    scratch = [
        VMEM((ns, 384, 2 * HEAD), BF),
        VMEM((blocks * 768, 2 * HEAD), BF),
        pltpu.SemaphoreType.DMA((len(arrays),)),
    ]
    if last:
        out_shape = [jax.ShapeDtypeStruct((ns, 8, 48, HEAD), BF)]
        scratch = scratch + [VMEM((ns, 384, HEAD), F32)] * 3
    else:
        out_shape = [jax.ShapeDtypeStruct((384, HEAD), F32)] * (3 * ns)
    units = blocks * ns * 17 / 64
    return pl.pallas_call(
        functools.partial(attend_kernel, parts, tuple(places), block0, blocks, first, last),
        out_shape=out_shape,
        in_specs=[pl.BlockSpec(memory_space=pltpu.SMEM)]
        + vmem_specs(1)
        + [pl.BlockSpec(memory_space=pl.ANY)] * len(arrays)
        + vmem_specs(len(state_in)),
        out_specs=vmem_specs(len(out_shape)),
        scratch_shapes=scratch,
        compiler_params=params(32),
        cost_estimate=pl.CostEstimate(
            flops=int(units * 1.3e9), bytes_accessed=8 << 20, transcendentals=int(units * 600000)
        ),
        name="attend",
    )(meta, q, *arrays, *state_in)


def project_kernel(meta, att_ref, *refs):
    w_refs, (o0, o1, o2, o3, w_scr, x_scr, sems) = refs[:7], refs[7:]
    copies, at = [], 0
    for j, w_ref in enumerate(w_refs):
        rows = w_ref.shape[0]
        copies.append(pltpu.make_async_copy(w_ref, w_scr.at[pl.ds(at, rows)], sems.at[j]))
        copies[j].start()
        at += rows
    k, p = meta[TEAM], meta[CORE]
    heads = [2 * k, 2 * k + 1]
    heads += [2 * (k ^ j) + p for j in (1, 2, 3)]
    heads += [2 * (k ^ j) + 1 - p for j in (1, 2, 3)]
    for i in range(4):
        for j, head in enumerate(heads):
            x_scr[48 * i : 48 * i + 48, j * HEAD : (j + 1) * HEAD] = att_ref[i, head]
    for copy in copies:
        copy.wait()
    for c0 in range(0, 2048, 512):
        cols = pl.ds(c0, 512)
        total = mm(x_scr[...], w_scr[:, cols])
        for i, o_ref in enumerate((o0, o1, o2, o3)):
            o_ref[:, cols] = total[48 * i : 48 * i + 48].astype(o_ref.dtype)


def project(meta, att, weights):
    sent = jax.ShapeDtypeStruct((48, 2048), BF)
    return pl.pallas_call(
        project_kernel,
        out_shape=[sent, sent, sent, jax.ShapeDtypeStruct((48, 2048), F32)],
        in_specs=[pl.BlockSpec(memory_space=pltpu.SMEM)]
        + vmem_specs(1)
        + [pl.BlockSpec(memory_space=pl.ANY)] * 7,
        out_specs=vmem_specs(4),
        scratch_shapes=[
            VMEM((1024, 2048), BF),
            VMEM((192, 1024), BF),
            pltpu.SemaphoreType.DMA((7,)),
        ],
        compiler_params=params(24),
        name="project",
    )(meta, att, *weights)


def row_fields(row):
    device = row >> 3
    ctx = device >> 4
    expert = ((device & 15) << 3) | (ctx >> 1)
    rank = ((ctx & 1) << 1) | ((row >> 2) & 1)
    return expert, rank, row & 3


def route_kernel(ids_ref, ids_t_ref, gates_ref, send_ref, high_ref, low_ref):
    ids, ids_t, gates = ids_ref[...], ids_t_ref[...], gates_ref[...]
    expert_lane = iota((48, 128), 1)
    named = jnp.zeros((48, 128), F32)
    gate = jnp.zeros((48, 128), F32)
    expert_row = iota((128, 48), 0)
    named_t = jnp.zeros((128, 48), F32)
    for k in range(8):
        hit = ids[:, k : k + 1] == expert_lane
        named = named + jnp.where(hit, 1.0, 0.0)
        gate = gate + jnp.where(hit, gates[:, k : k + 1], 0.0)
        named_t = named_t + jnp.where(ids_t[k : k + 1, :] == expert_row, 1.0, 0.0)
    lower = jnp.where(iota((48, 48), 1) <= iota((48, 48), 0), 1.0, 0.0).astype(BF)
    upper = jnp.where(iota((48, 48), 0) <= iota((48, 48), 1), 1.0, 0.0).astype(BF)
    rank = (mm(lower, named.astype(BF)) * named).astype(BF)
    rank_t = (mm(named_t.astype(BF), upper) * named_t).astype(BF)
    high = gate.astype(BF)
    low = (gate - high.astype(F32)).astype(BF)

    expert, want, quarter = row_fields(iota((2048, 128), 0))
    pick = jnp.where(expert == iota((2048, 128), 1), 1.0, 0.0).astype(BF)
    have = mm(pick, rank_t)
    expert, want, quarter = row_fields(iota((2048, 48), 0))
    wanted = (want + 1).astype(F32)
    parts = [jnp.where((have == wanted) & (quarter == q), 1.0, 0.0) for q in range(4)]
    for q in range(4):
        send_ref[:, 48 * q : 48 * q + 48] = parts[q].astype(BF)

    expert, want, quarter = row_fields(iota((128, 2048), 1))
    pick = jnp.where(expert == iota((128, 2048), 0), 1.0, 0.0).astype(BF)
    have = mm(rank, pick)
    got_high, got_low = mm(high, pick), mm(low, pick)
    expert, want, quarter = row_fields(iota((48, 2048), 1))
    live = have == (want + 1).astype(F32)
    for q in range(4):
        here = live & (quarter == q)
        sl = pl.ds(48 * q, 48)
        high_ref[sl, :] = jnp.where(here, got_high, 0.0).astype(BF)
        low_ref[sl, :] = jnp.where(here, got_low, 0.0).astype(BF)


def route(ids, gates):
    back = jax.ShapeDtypeStruct((192, 2048), BF)
    return pl.pallas_call(
        route_kernel,
        out_shape=[jax.ShapeDtypeStruct((2048, 192), BF), back, back],
        in_specs=vmem_specs(3),
        out_specs=vmem_specs(3),
        compiler_params=params(24),
        cost_estimate=pl.CostEstimate(
            flops=400 << 20, bytes_accessed=3 << 20, transcendentals=0
        ),
        name="route",
    )(ids, ids.T, gates)


def dispatch_kernel(
    residual, own, r1, r2, r3, gain, send, mixed_ref, out_ref, stack, rows_scr, sems
):
    mixed = residual[...].astype(F32) + own[...]
    mixed = mixed + r1[...].astype(F32) + r2[...].astype(F32) + r3[...].astype(F32)
    mixed_ref[...] = mixed
    mean_square = jnp.mean(mixed * mixed, axis=-1, keepdims=True)
    normed = (mixed * lax.rsqrt(mean_square + 1e-06) * gain[...]).astype(BF)
    for q in range(4):
        stack[48 * q : 48 * q + 48, :] = normed[:, 512 * q : 512 * q + 512]
    copies = []
    for i in range(8):
        sl = pl.ds(i * 256, 256)
        rows_scr[sl, :] = mm(send[sl, :], stack[...]).astype(BF)
        copy = pltpu.make_async_copy(rows_scr.at[sl], out_ref.at[sl], sems.at[i])
        copy.start()
        copies.append(copy)
    for copy in copies:
        copy.wait()


def dispatch(residual, own, received, gain, send):
    return pl.pallas_call(
        dispatch_kernel,
        out_shape=[
            jax.ShapeDtypeStruct((48, 2048), F32),
            jax.ShapeDtypeStruct((2048, 512), BF),
        ],
        in_specs=vmem_specs(7),
        out_specs=vmem_specs(1) + [pl.BlockSpec(memory_space=pltpu.HBM)],
        scratch_shapes=[
            VMEM((192, 512), BF),
            VMEM((2048, 512), BF),
            pltpu.SemaphoreType.DMA((8,)),
        ],
        compiler_params=params(24),
        name="dispatch",
    )(residual, own, *received, gain, send)


def combine_kernel(mixed, high, low, results, out_ref):
    total = mm(high[...], results[...]) + mm(low[...], results[...])
    for q in range(4):
        cols = pl.ds(512 * q, 512)
        out_ref[:, cols] = (mixed[:, cols] + total[48 * q : 48 * q + 48]).astype(BF)


def combine(mixed, high, low, results):
    return pl.pallas_call(
        combine_kernel,
        out_shape=jax.ShapeDtypeStruct((48, 2048), BF),
        in_specs=vmem_specs(4),
        out_specs=pl.BlockSpec(memory_space=VMEM),
        compiler_params=params(24),
        name="combine",
    )(mixed, high, low, results)


def expert_kernel(
    rows_ref,
    g0,
    u0,
    d0,
    g1,
    u1,
    d1,
    out_ref,
    in_scr,
    out_scr,
    x_scr,
    hidden_scr,
    y_scr,
    gate_scr,
    up_scr,
    down_scr,
    sems,
    in_sems,
    out_sems,
):
    def block_in(b):
        sl = pl.ds(b * 256, 256)
        return pltpu.make_async_copy(rows_ref.at[sl], in_scr.at[sl], in_sems.at[b])

    def block_out(b):
        sl = pl.ds(b * 256, 256)
        return pltpu.make_async_copy(out_scr.at[sl], out_ref.at[sl], out_sems.at[b])

    for b in range(8):
        block_in(b).start()
    copies = []
    for i, (g, u, d) in enumerate(((g0, u0, d0), (g1, u1, d1))):
        part = pl.ds(384 * i, 384)
        copies.append(pltpu.make_async_copy(g, gate_scr.at[:, part], sems.at[3 * i]))
        copies.append(pltpu.make_async_copy(u, up_scr.at[:, part], sems.at[3 * i + 1]))
        copies.append(pltpu.make_async_copy(d, down_scr.at[part], sems.at[3 * i + 2]))
    for i in (0, 1, 3, 4, 2, 5):
        copies[i].start()
    to_row, from_col = iota((256, 256), 0), iota((256, 256), 1)
    sort = jnp.where(from_col == ((to_row & 63) << 2) + (to_row >> 6), 1.0, 0.0).astype(BF)
    unsort = jnp.where(to_row == ((from_col & 63) << 2) + (from_col >> 6), 1.0, 0.0).astype(BF)

    for b in range(8):
        block_in(b).wait()
        block = mm(sort, in_scr[256 * b : 256 * b + 256, :]).astype(BF)
        for q in range(4):
            x_scr[64 * b : 64 * b + 64, 512 * q : 512 * q + 512] = block[64 * q : 64 * q + 64]
    for j in range(3):
        if j < 2:
            copies[3 * j].wait()
            copies[3 * j + 1].wait()
        cols = pl.ds(256 * j, 256)

        gate = mm(x_scr[...], gate_scr[:, cols])
        up = mm(x_scr[...], up_scr[:, cols])
        hidden_scr[:, cols] = (gate / (1.0 + jnp.exp(-gate)) * up).astype(BF)
    copies[2].wait()
    copies[5].wait()
    for q in range(4):
        part = mm(hidden_scr[...], down_scr[:, 512 * q : 512 * q + 512])
        y_scr[q] = part.astype(BF)
    for b in range(8):
        tokens = pl.ds(64 * b, 64)
        block = jnp.concatenate([y_scr[q, tokens, :] for q in range(4)], axis=0)
        out_scr[256 * b : 256 * b + 256, :] = mm(unsort, block).astype(BF)
        block_out(b).start()
    for b in range(8):
        block_out(b).wait()


def experts(rows, weights):
    return pl.pallas_call(
        expert_kernel,
        out_shape=jax.ShapeDtypeStruct((2048, 512), BF),
        in_specs=[pl.BlockSpec(memory_space=pltpu.HBM)] * 7,
        out_specs=pl.BlockSpec(memory_space=pltpu.HBM),
        scratch_shapes=[
            VMEM((2048, 512), BF),
            VMEM((2048, 512), BF),
            VMEM((512, 2048), BF),
            VMEM((512, 768), BF),
            VMEM((4, 512, 512), BF),
            VMEM((2048, 768), BF),
            VMEM((2048, 768), BF),
            VMEM((768, 2048), BF),
            pltpu.SemaphoreType.DMA((6,)),
            pltpu.SemaphoreType.DMA((8,)),
            pltpu.SemaphoreType.DMA((8,)),
        ],
        compiler_params=params(60),
        name="experts",
    )(rows, *weights)


def along_ctx(x, source_of):
    return lax.ppermute(x, "ctx", [(source_of(c), c) for c in range(16)])


def along_exp(x, flip):
    return lax.ppermute(x, "exp", [(e ^ flip, e) for e in range(16)])


def along_both(x, mirror, flip):
    pairs = [
        (c * 16 + e, ((15 - c) if mirror else c) * 16 + (e ^ flip))
        for c in range(16)
        for e in range(16)
    ]
    return lax.ppermute(x, ("ctx", "exp"), pairs)


def local(
    queries,
    keys,
    values,
    out_weight,
    residual,
    norm_gain,
    route_ids,
    route_gates,
    w_gate,
    w_up,
    w_down,
):
    c = lax.axis_index("ctx")
    e = lax.axis_index("exp")
    core, g, k = c % 2, e // 4, e % 4
    pair = g // 2

    kv_head = e // 8
    own = jnp.concatenate(
        [
            lax.dynamic_slice_in_dim(keys, kv_head * HEAD, HEAD, 1),
            lax.dynamic_slice_in_dim(values, kv_head * HEAD, HEAD, 1),
        ],
        axis=1,
    )

    def swap(x):
        return along_ctx(x, lambda i: i ^ 1)

    def from_y(x):
        return along_ctx(x, lambda i: i ^ 2)

    def from_x(x, step):
        return along_ctx(x, lambda i: (i + 4 * step) % 16)

    n1, n2, n3 = from_x(own, 1), from_x(own, -1), from_y(own)
    x, y = c // 4, (c // 2) % 2

    def ctx_of(dx, dy, dp):
        return ((x + dx) % 4) * 4 + (y ^ dy) * 2 + (core ^ dp)

    high_ctx = (c >= 8).astype(jnp.int32)
    grouped = queries.reshape(2, 2, 4, 48, 256).transpose(0, 2, 1, 3, 4)
    outgoing = jnp.where((pair + high_ctx) % 2 == 0, grouped, grouped[::-1])
    teams = [
        [cc * 16 + gg * 4 + kk for cc in (low, 15 - low) for kk in range(4)]
        for low in range(8)
        for gg in range(4)
    ]
    q = lax.all_to_all(
        outgoing.reshape(8, 2, 48, 256),
        ("ctx", "exp"),
        split_axis=0,
        concat_axis=0,
        tiled=True,
        axis_index_groups=teams,
    ).reshape(2, 4, 2, 48, 256)
    w_part = lax.dynamic_slice_in_dim(out_weight, core * HEAD, HEAD, 0)

    w1 = lax.ppermute(
        w_part,
        ("ctx", "exp"),
        [(i * 16 + j, (i ^ 2) * 16 + (j ^ 1)) for i in range(16) for j in range(16)],
    )

    near = [(0, 0), (1, 0), (3, 0), (0, 1)]
    far = [(2, 0), (3, 1), (1, 1), (2, 1)]
    order = [(dx, dy, dp) for half in (near, far) for dp in (0, 1) for dx, dy in half]
    odd = g % 2
    halves = [odd, 1 - odd, 1 - odd, odd]
    pairs = [1 - pair, pair, 1 - pair, pair]
    bases = [((2 * pp + half) * 4 + k) * 48 for pp, half in zip(pairs, halves)]
    meta = jnp.stack(
        [15 - c, c] + bases + halves + [1 - high_ctx, high_ctx, k, core] + [ctx_of(*place) for place in order]
    ).astype(jnp.int32)

    w2 = along_exp(w_part, 2)
    n1, n2, n3, q, w1, w2, meta = lax.optimization_barrier((n1, n2, n3, q, w1, w2, meta))
    s_near = swap(jnp.concatenate([own, n1, n2, n3], axis=0))
    w3 = along_exp(w1, 2)
    n4, n5, n6 = from_x(n1, 1), from_x(n3, -1), from_y(n1)
    n7 = along_ctx(own, lambda i: (i ^ 2) ^ 8)
    parts = (0, 1, 2, 3)
    places = [(i, 0, 768) for i in range(4)] + [(4, 0, 3072)]
    state = attend(parts, meta, q, [own, n1, n2, n3, s_near], places, 0, None)

    state, n4, n5, n6, n7, w3 = lax.optimization_barrier((state, n4, n5, n6, n7, w3))
    s_far = swap(jnp.concatenate([n4, n5, n6, n7], axis=0))
    (attended,) = attend(parts, meta, q, [n4, n5, n6, n7, s_far], places, 8, state)
    weights = [out_weight, w1, w2, w3] + [swap(w) for w in (w1, w2, w3)]
    t2, t1, t3, mine = project(meta, attended, weights)
    received = [along_both(t2, True, 8), along_both(t3, True, 12), along_both(t1, False, 4)]

    send, back_high, back_low = route(route_ids, route_gates)
    mixed, rows = dispatch(residual, mine, received, norm_gain[None, :], send)

    own_w = [w_gate[0, 0], w_up[0, 0], w_down[0, 0]]
    other_w = [swap(w) for w in own_w]

    def exchange(v):
        return lax.all_to_all(
            v.reshape(256, 8, 512), ("ctx", "exp"), split_axis=0, concat_axis=0, tiled=True
        ).reshape(2048, 512)

    results = exchange(experts(exchange(rows), own_w + other_w))
    return combine(mixed, back_high, back_low, results)


def solution(mesh):
    placed = (
        P("ctx", "exp"),
        P("ctx", None),
        P("ctx", None),
        P("exp", None),
        P(("ctx", "exp"), None),
        P(),
        P(("ctx", "exp"), None),
        P(("ctx", "exp"), None),
        P("ctx", "exp", None, None),
        P("ctx", "exp", None, None),
        P("ctx", "exp", None, None),
    )
    return jax.shard_map(
        local, mesh=mesh, in_specs=placed, out_specs=P(("ctx", "exp"), None), check_vma=False
    )
```

```python
import functools
import math

import jax
import jax.numpy as jnp
import numpy as np
from jax import lax
from jax.experimental import pallas as pl
from jax.experimental.pallas import tpu as pltpu
from jax.sharding import PartitionSpec as P

HEAD = 128
NEG = -1e30
BF = jnp.bfloat16
F32 = jnp.float32
VMEM = pltpu.VMEM
MIB = 1 << 20


def params(mib):
    return pltpu.CompilerParams(vmem_limit_bytes=mib * MIB)


def vmem_specs(count):
    return [pl.BlockSpec(memory_space=VMEM)] * count


def mm(a, b):
    return jnp.dot(a, b, preferred_element_type=F32)


SET_CTX, BASE, HALF, PLACE, TEAM, CORE, BLOCK_CTX = 0, 2, 6, 10, 12, 13, 14


def iota(shape, dim):
    return lax.broadcasted_iota(jnp.int32, shape, dim)


def attend_rows(tiles, keys2, values1, bases):
    width = keys2.shape[0]
    scores = []
    for i, tile in enumerate(tiles):
        part = lax.dot_general(
            tile[0][...], keys2, (((1,), (1,)), ((), ())), preferred_element_type=F32
        )
        if bases is not None:
            row = iota((384, 1), 0)
            q_pos = bases[i] + row - 48 * ((row * 1366) >> 16)
            part = jnp.where(iota((384, width), 1) <= q_pos, part, NEG)
        scores.append(part)
    terms, maxima = [], []
    for part, (_, m_ref, _, _) in zip(scores, tiles):
        m_old = m_ref[...]
        m_new = jnp.maximum(m_old, jnp.max(part, axis=1, keepdims=True))
        wide = jnp.concatenate([m_new] * (width // 128), axis=1)
        terms.append(jnp.exp2(part - wide).astype(BF))
        maxima.append((m_old, m_new))
    for part, (m_old, m_new), (_, m_ref, l_ref, a_ref) in zip(terms, maxima, tiles):
        update = mm(part, values1)
        shrink = jnp.exp2(m_old - m_new)
        a_ref[...] = a_ref[...] * shrink + update[:, :HEAD]
        l_ref[...] = l_ref[...] * shrink + update[:, HEAD:]
        m_ref[...] = m_new


def attend_kernel(parts, places, block0, blocks, first, last, meta, *refs):
    n, ns = len(places), len(parts)
    q_ref, refs = refs[0], refs[1:]
    kv_refs, refs = refs[:n], refs[n:]
    if not first:
        state_in, refs = refs[: 3 * ns], refs[3 * ns :]
    if last:
        o_ref, q_scr, kv_scr, sems, m_scr, l_scr, a_scr = refs
        state = [(m_scr.at[i], l_scr.at[i], a_scr.at[i]) for i in range(ns)]
    else:
        q_scr, kv_scr, sems = refs[3 * ns :]
        state = [tuple(refs[3 * i : 3 * i + 3]) for i in range(ns)]
    copies = []
    for i, (kv_ref, (block, start, rows)) in enumerate(zip(kv_refs, places)):
        copy = pltpu.make_async_copy(
            kv_ref, kv_scr.at[pl.ds(block * 768 + start, rows)], sems.at[i]
        )
        copy.start()
        copies.append(copy)
    scale = np.float32(math.log2(math.e) / math.sqrt(HEAD))
    for i, part in enumerate(parts):
        half, place = meta[HALF + part], meta[PLACE + part % 2]
        for k in range(4):
            for p in range(2):
                q = q_ref[place, k, half, :, p * HEAD : (p + 1) * HEAD].astype(F32) * scale
                high = q.astype(BF)
                low = (q - high.astype(F32)).astype(BF)
                sl = pl.ds((2 * k + p) * 48, 48)
                q_scr[i, sl, :HEAD] = high
                q_scr[i, sl, HEAD:] = low
        m_ref, l_ref, a_ref = state[i]
        if first:
            m_ref[...] = jnp.full(m_ref.shape, NEG, F32)
            l_ref[...] = jnp.zeros(l_ref.shape, F32)
            a_ref[...] = jnp.zeros(a_ref.shape, F32)
        else:
            for dst, src in zip(state[i], state_in[3 * i : 3 * i + 3]):
                dst[...] = src[...]
    mirror = [i for i in range(ns) if parts[i] % 2 == 0]
    own = [i for i in range(ns) if parts[i] % 2 == 1]
    mirror_ctx, own_ctx = meta[SET_CTX], meta[SET_CTX + 1]

    def step(j, carry):
        for copy, (block, _, _) in zip(copies, places):
            pl.when(j == block)(copy.wait)
        block_ctx = meta[BLOCK_CTX + block0 + j]
        sl = pl.ds(pl.multiple_of(j * 768, 768), 768)

        def run(chosen, masked):
            k = kv_scr[sl, :HEAD]
            v = kv_scr[sl, HEAD:]
            keys2 = jnp.concatenate([k, k], axis=1)
            values1 = jnp.concatenate([v, jnp.ones_like(v)], axis=1)
            tiles = [(q_scr.at[i],) + state[i] for i in chosen]
            bases = [meta[BASE + parts[i]] for i in chosen] if masked else None
            attend_rows(tiles, keys2, values1, bases)

        to_mirror, to_own = block_ctx < mirror_ctx, block_ctx < own_ctx
        pl.when(to_mirror & to_own)(lambda: run(mirror + own, False))
        pl.when(to_mirror & jnp.logical_not(to_own))(lambda: run(mirror, False))
        pl.when(to_own & jnp.logical_not(to_mirror))(lambda: run(own, False))
        pl.when(block_ctx == mirror_ctx)(lambda: run(mirror, True))
        pl.when(block_ctx == own_ctx)(lambda: run(own, True))
        return carry

    lax.fori_loop(0, blocks, step, 0)
    if last:
        o_ref[...] = (a_scr[...] / l_scr[...]).astype(BF).reshape(o_ref.shape)


def attend(parts, meta, q, arrays, places, block0, state):
    ns, first, last = len(parts), state is None, state is not None
    blocks = max(p[0] + (p[1] + p[2] + 767) // 768 for p in places)
    state_in = () if first else tuple(state)
    scratch = [
        VMEM((ns, 384, 2 * HEAD), BF),
        VMEM((blocks * 768, 2 * HEAD), BF),
        pltpu.SemaphoreType.DMA((len(arrays),)),
    ]
    if last:
        out_shape = [jax.ShapeDtypeStruct((ns, 8, 48, HEAD), BF)]
        scratch = scratch + [VMEM((ns, 384, HEAD), F32)] * 3
    else:
        out_shape = [jax.ShapeDtypeStruct((384, HEAD), F32)] * (3 * ns)
    units = blocks * ns * 17 / 64
    return pl.pallas_call(
        functools.partial(attend_kernel, parts, tuple(places), block0, blocks, first, last),
        out_shape=out_shape,
        in_specs=[pl.BlockSpec(memory_space=pltpu.SMEM)]
        + vmem_specs(1)
        + [pl.BlockSpec(memory_space=pl.ANY)] * len(arrays)
        + vmem_specs(len(state_in)),
        out_specs=vmem_specs(len(out_shape)),
        scratch_shapes=scratch,
        compiler_params=params(32),
        cost_estimate=pl.CostEstimate(
            flops=int(units * 1.3e9), bytes_accessed=8 << 20, transcendentals=int(units * 600000)
        ),
        name="attend",
    )(meta, q, *arrays, *state_in)


def project_kernel(meta, att_ref, *refs):
    w_refs, (o0, o1, o2, o3, w_scr, x_scr, sems) = refs[:7], refs[7:]
    copies, at = [], 0
    for j, w_ref in enumerate(w_refs):
        rows = w_ref.shape[0]
        copies.append(pltpu.make_async_copy(w_ref, w_scr.at[pl.ds(at, rows)], sems.at[j]))
        copies[j].start()
        at += rows
    k, p = meta[TEAM], meta[CORE]
    heads = [2 * k, 2 * k + 1]
    heads += [2 * (k ^ j) + p for j in (1, 2, 3)]
    heads += [2 * (k ^ j) + 1 - p for j in (1, 2, 3)]
    for i in range(4):
        for j, head in enumerate(heads):
            x_scr[48 * i : 48 * i + 48, j * HEAD : (j + 1) * HEAD] = att_ref[i, head]
    for copy in copies:
        copy.wait()
    for c0 in range(0, 2048, 512):
        cols = pl.ds(c0, 512)
        total = mm(x_scr[...], w_scr[:, cols])
        for i, o_ref in enumerate((o0, o1, o2, o3)):
            o_ref[:, cols] = total[48 * i : 48 * i + 48].astype(o_ref.dtype)


def project(meta, att, weights):
    sent = jax.ShapeDtypeStruct((48, 2048), BF)
    return pl.pallas_call(
        project_kernel,
        out_shape=[sent, sent, sent, jax.ShapeDtypeStruct((48, 2048), F32)],
        in_specs=[pl.BlockSpec(memory_space=pltpu.SMEM)]
        + vmem_specs(1)
        + [pl.BlockSpec(memory_space=pl.ANY)] * 7,
        out_specs=vmem_specs(4),
        scratch_shapes=[
            VMEM((1024, 2048), BF),
            VMEM((192, 1024), BF),
            pltpu.SemaphoreType.DMA((7,)),
        ],
        compiler_params=params(24),
        name="project",
    )(meta, att, *weights)


def row_fields(row):
    device = row >> 3
    ctx = device >> 4
    expert = ((device & 15) << 3) | (ctx >> 1)
    rank = ((ctx & 1) << 1) | ((row >> 2) & 1)
    return expert, rank, row & 3


def route_kernel(ids_ref, ids_t_ref, gates_ref, send_ref, high_ref, low_ref):
    ids, ids_t, gates = ids_ref[...], ids_t_ref[...], gates_ref[...]
    expert_lane = iota((48, 128), 1)
    named = jnp.zeros((48, 128), F32)
    gate = jnp.zeros((48, 128), F32)
    expert_row = iota((128, 48), 0)
    named_t = jnp.zeros((128, 48), F32)
    for k in range(8):
        hit = ids[:, k : k + 1] == expert_lane
        named = named + jnp.where(hit, 1.0, 0.0)
        gate = gate + jnp.where(hit, gates[:, k : k + 1], 0.0)
        named_t = named_t + jnp.where(ids_t[k : k + 1, :] == expert_row, 1.0, 0.0)
    lower = jnp.where(iota((48, 48), 1) <= iota((48, 48), 0), 1.0, 0.0).astype(BF)
    upper = jnp.where(iota((48, 48), 0) <= iota((48, 48), 1), 1.0, 0.0).astype(BF)
    rank = (mm(lower, named.astype(BF)) * named).astype(BF)
    rank_t = (mm(named_t.astype(BF), upper) * named_t).astype(BF)
    high = gate.astype(BF)
    low = (gate - high.astype(F32)).astype(BF)

    expert, want, quarter = row_fields(iota((2048, 128), 0))
    pick = jnp.where(expert == iota((2048, 128), 1), 1.0, 0.0).astype(BF)
    have = mm(pick, rank_t)
    expert, want, quarter = row_fields(iota((2048, 48), 0))
    wanted = (want + 1).astype(F32)
    parts = [jnp.where((have == wanted) & (quarter == q), 1.0, 0.0) for q in range(4)]
    for q in range(4):
        send_ref[:, 48 * q : 48 * q + 48] = parts[q].astype(BF)

    expert, want, quarter = row_fields(iota((128, 2048), 1))
    pick = jnp.where(expert == iota((128, 2048), 0), 1.0, 0.0).astype(BF)
    have = mm(rank, pick)
    got_high, got_low = mm(high, pick), mm(low, pick)
    expert, want, quarter = row_fields(iota((48, 2048), 1))
    live = have == (want + 1).astype(F32)
    for q in range(4):
        here = live & (quarter == q)
        sl = pl.ds(48 * q, 48)
        high_ref[sl, :] = jnp.where(here, got_high, 0.0).astype(BF)
        low_ref[sl, :] = jnp.where(here, got_low, 0.0).astype(BF)


def route(ids, gates):
    back = jax.ShapeDtypeStruct((192, 2048), BF)
    return pl.pallas_call(
        route_kernel,
        out_shape=[jax.ShapeDtypeStruct((2048, 192), BF), back, back],
        in_specs=vmem_specs(3),
        out_specs=vmem_specs(3),
        compiler_params=params(24),
        cost_estimate=pl.CostEstimate(
            flops=400 << 20, bytes_accessed=3 << 20, transcendentals=0
        ),
        name="route",
    )(ids, ids.T, gates)


def dispatch_kernel(
    residual, own, r1, r2, r3, r4, gain, send, mixed_ref, out_ref, stack, rows_scr, sems
):
    mixed = residual[...].astype(F32) + own[...]
    r14 = jnp.concatenate([r1[...], r4[...]], axis=1)
    mixed = mixed + r14.astype(F32) + r2[...].astype(F32) + r3[...].astype(F32)
    mixed_ref[...] = mixed
    mean_square = jnp.mean(mixed * mixed, axis=-1, keepdims=True)
    normed = (mixed * lax.rsqrt(mean_square + 1e-06) * gain[...]).astype(BF)
    for q in range(4):
        stack[48 * q : 48 * q + 48, :] = normed[:, 512 * q : 512 * q + 512]
    copies = []
    for i in range(8):
        sl = pl.ds(i * 256, 256)
        rows_scr[sl, :] = mm(send[sl, :], stack[...]).astype(BF)
        copy = pltpu.make_async_copy(rows_scr.at[sl], out_ref.at[sl], sems.at[i])
        copy.start()
        copies.append(copy)
    for copy in copies:
        copy.wait()


def dispatch(residual, own, received, gain, send):
    return pl.pallas_call(
        dispatch_kernel,
        out_shape=[
            jax.ShapeDtypeStruct((48, 2048), F32),
            jax.ShapeDtypeStruct((2048, 512), BF),
        ],
        in_specs=vmem_specs(8),
        out_specs=vmem_specs(1) + [pl.BlockSpec(memory_space=pltpu.HBM)],
        scratch_shapes=[
            VMEM((192, 512), BF),
            VMEM((2048, 512), BF),
            pltpu.SemaphoreType.DMA((8,)),
        ],
        compiler_params=params(24),
        name="dispatch",
    )(residual, own, *received, gain, send)


def combine_kernel(mixed, high, low, results, out_ref):
    total = mm(high[...], results[...]) + mm(low[...], results[...])
    for q in range(4):
        cols = pl.ds(512 * q, 512)
        out_ref[:, cols] = (mixed[:, cols] + total[48 * q : 48 * q + 48]).astype(BF)


def combine(mixed, high, low, results):
    return pl.pallas_call(
        combine_kernel,
        out_shape=jax.ShapeDtypeStruct((48, 2048), BF),
        in_specs=vmem_specs(4),
        out_specs=pl.BlockSpec(memory_space=VMEM),
        compiler_params=params(24),
        name="combine",
    )(mixed, high, low, results)


def expert_kernel(
    rows_ref,
    g0,
    u0,
    d0,
    g1,
    u1,
    d1,
    out_ref,
    in_scr,
    out_scr,
    x_scr,
    hidden_scr,
    y_scr,
    gate_scr,
    up_scr,
    down_scr,
    sems,
    in_sems,
    out_sems,
):
    def block_in(b):
        sl = pl.ds(b * 256, 256)
        return pltpu.make_async_copy(rows_ref.at[sl], in_scr.at[sl], in_sems.at[b])

    def block_out(b):
        sl = pl.ds(b * 256, 256)
        return pltpu.make_async_copy(out_scr.at[sl], out_ref.at[sl], out_sems.at[b])

    for b in range(8):
        block_in(b).start()
    copies = []
    for i, (g, u, d) in enumerate(((g0, u0, d0), (g1, u1, d1))):
        part = pl.ds(384 * i, 384)
        copies.append(pltpu.make_async_copy(g, gate_scr.at[:, part], sems.at[3 * i]))
        copies.append(pltpu.make_async_copy(u, up_scr.at[:, part], sems.at[3 * i + 1]))
        copies.append(pltpu.make_async_copy(d, down_scr.at[part], sems.at[3 * i + 2]))
    for i in (0, 1, 3, 4, 2, 5):
        copies[i].start()
    to_row, from_col = iota((256, 256), 0), iota((256, 256), 1)
    sort = jnp.where(from_col == ((to_row & 63) << 2) + (to_row >> 6), 1.0, 0.0).astype(BF)
    unsort = jnp.where(to_row == ((from_col & 63) << 2) + (from_col >> 6), 1.0, 0.0).astype(BF)

    for b in range(8):
        block_in(b).wait()
        block = mm(sort, in_scr[256 * b : 256 * b + 256, :]).astype(BF)
        for q in range(4):
            x_scr[64 * b : 64 * b + 64, 512 * q : 512 * q + 512] = block[64 * q : 64 * q + 64]
    for j in range(3):
        if j < 2:
            copies[3 * j].wait()
            copies[3 * j + 1].wait()
        cols = pl.ds(256 * j, 256)

        gate = mm(x_scr[...], gate_scr[:, cols])
        up = mm(x_scr[...], up_scr[:, cols])
        hidden_scr[:, cols] = (gate / (1.0 + jnp.exp(-gate)) * up).astype(BF)
    copies[2].wait()
    copies[5].wait()
    for q in range(4):
        part = mm(hidden_scr[...], down_scr[:, 512 * q : 512 * q + 512])
        y_scr[q] = part.astype(BF)
    for b in range(8):
        tokens = pl.ds(64 * b, 64)
        block = jnp.concatenate([y_scr[q, tokens, :] for q in range(4)], axis=0)
        out_scr[256 * b : 256 * b + 256, :] = mm(unsort, block).astype(BF)
        block_out(b).start()
    for b in range(8):
        block_out(b).wait()


def experts(rows, weights):
    return pl.pallas_call(
        expert_kernel,
        out_shape=jax.ShapeDtypeStruct((2048, 512), BF),
        in_specs=[pl.BlockSpec(memory_space=pltpu.HBM)] * 7,
        out_specs=pl.BlockSpec(memory_space=pltpu.HBM),
        scratch_shapes=[
            VMEM((2048, 512), BF),
            VMEM((2048, 512), BF),
            VMEM((512, 2048), BF),
            VMEM((512, 768), BF),
            VMEM((4, 512, 512), BF),
            VMEM((2048, 768), BF),
            VMEM((2048, 768), BF),
            VMEM((768, 2048), BF),
            pltpu.SemaphoreType.DMA((6,)),
            pltpu.SemaphoreType.DMA((8,)),
            pltpu.SemaphoreType.DMA((8,)),
        ],
        compiler_params=params(60),
        name="experts",
    )(rows, *weights)


def along_ctx(x, source_of):
    return lax.ppermute(x, "ctx", [(source_of(c), c) for c in range(16)])


def along_exp(x, flip):
    return lax.ppermute(x, "exp", [(e ^ flip, e) for e in range(16)])


def along_both(x, mirror, flip):
    pairs = [
        (c * 16 + e, ((15 - c) if mirror else c) * 16 + (e ^ flip))
        for c in range(16)
        for e in range(16)
    ]
    return lax.ppermute(x, ("ctx", "exp"), pairs)


def rotate(x, mirror):
    pairs = [
        (c * 16 + e, ((15 - c) if mirror else c) * 16 + (e - 4) % 16)
        for c in range(16)
        for e in range(16)
    ]
    return lax.ppermute(x, ("ctx", "exp"), pairs)


def local(
    queries,
    keys,
    values,
    out_weight,
    residual,
    norm_gain,
    route_ids,
    route_gates,
    w_gate,
    w_up,
    w_down,
):
    c = lax.axis_index("ctx")
    e = lax.axis_index("exp")
    core, g, k = c % 2, e // 4, e % 4
    pair = g // 2

    kv_head = e // 8
    own = jnp.concatenate(
        [
            lax.dynamic_slice_in_dim(keys, kv_head * HEAD, HEAD, 1),
            lax.dynamic_slice_in_dim(values, kv_head * HEAD, HEAD, 1),
        ],
        axis=1,
    )

    def swap(x):
        return along_ctx(x, lambda i: i ^ 1)

    def from_y(x):
        return along_ctx(x, lambda i: i ^ 2)

    def from_x(x, step):
        return along_ctx(x, lambda i: (i + 4 * step) % 16)

    n1, n2, n3 = from_x(own, 1), from_x(own, -1), from_y(own)
    x, y = c // 4, (c // 2) % 2

    def ctx_of(dx, dy, dp):
        return ((x + dx) % 4) * 4 + (y ^ dy) * 2 + (core ^ dp)

    high_ctx = (c >= 8).astype(jnp.int32)
    grouped = queries.reshape(2, 2, 4, 48, 256).transpose(0, 2, 1, 3, 4)
    outgoing = jnp.where((pair + high_ctx) % 2 == 0, grouped, grouped[::-1])
    teams = [
        [cc * 16 + gg * 4 + kk for cc in (low, 15 - low) for kk in range(4)]
        for low in range(8)
        for gg in range(4)
    ]
    q = lax.all_to_all(
        outgoing.reshape(8, 2, 48, 256),
        ("ctx", "exp"),
        split_axis=0,
        concat_axis=0,
        tiled=True,
        axis_index_groups=teams,
    ).reshape(2, 4, 2, 48, 256)
    w_part = lax.dynamic_slice_in_dim(out_weight, core * HEAD, HEAD, 0)

    w1 = lax.ppermute(
        w_part,
        ("ctx", "exp"),
        [(i * 16 + j, (i ^ 2) * 16 + (j ^ 1)) for i in range(16) for j in range(16)],
    )

    near = [(0, 0), (1, 0), (3, 0), (0, 1)]
    far = [(2, 0), (3, 1), (1, 1), (2, 1)]
    order = [(dx, dy, dp) for half in (near, far) for dp in (0, 1) for dx, dy in half]
    odd = g % 2
    halves = [odd, 1 - odd, 1 - odd, odd]
    pairs = [1 - pair, pair, 1 - pair, pair]
    bases = [((2 * pp + half) * 4 + k) * 48 for pp, half in zip(pairs, halves)]
    meta = jnp.stack(
        [15 - c, c] + bases + halves + [1 - high_ctx, high_ctx, k, core] + [ctx_of(*place) for place in order]
    ).astype(jnp.int32)

    w2 = along_exp(w_part, 2)
    n1, n2, n3, q, w1, w2, meta = lax.optimization_barrier((n1, n2, n3, q, w1, w2, meta))
    s_near = swap(jnp.concatenate([own, n1, n2, n3], axis=0))
    w3 = along_exp(w1, 2)
    n4, n5, n6 = from_x(n1, 1), from_x(n3, -1), from_y(n1)
    n7 = along_ctx(own, lambda i: (i ^ 2) ^ 8)
    parts = (0, 1, 2, 3)
    places = [(i, 0, 768) for i in range(4)] + [(4, 0, 3072)]
    state = attend(parts, meta, q, [own, n1, n2, n3, s_near], places, 0, None)

    state, n4, n5, n6, n7, w3 = lax.optimization_barrier((state, n4, n5, n6, n7, w3))
    s_far = swap(jnp.concatenate([n4, n5, n6, n7], axis=0))
    (attended,) = attend(parts, meta, q, [n4, n5, n6, n7, s_far], places, 8, state)
    weights = [out_weight, w1, w2, w3] + [swap(w) for w in (w1, w2, w3)]
    t2, t1, t3, mine = project(meta, attended, weights)
    back = rotate(t2[:, 1024:], False)
    received = [along_both(t2[:, :1024], True, 8), along_both(t3, True, 12)]
    received += [along_both(t1, False, 4), rotate(back, True)]

    send, back_high, back_low = route(route_ids, route_gates)
    mixed, rows = dispatch(residual, mine, received, norm_gain[None, :], send)

    own_w = [w_gate[0, 0], w_up[0, 0], w_down[0, 0]]
    other_w = [swap(w) for w in own_w]

    def exchange(v):
        return lax.all_to_all(
            v.reshape(256, 8, 512), ("ctx", "exp"), split_axis=0, concat_axis=0, tiled=True
        ).reshape(2048, 512)

    results = exchange(experts(exchange(rows), own_w + other_w))
    return combine(mixed, back_high, back_low, results)


def solution(mesh):
    placed = (
        P("ctx", "exp"),
        P("ctx", None),
        P("ctx", None),
        P("exp", None),
        P(("ctx", "exp"), None),
        P(),
        P(("ctx", "exp"), None),
        P(("ctx", "exp"), None),
        P("ctx", "exp", None, None),
        P("ctx", "exp", None, None),
        P("ctx", "exp", None, None),
    )
    return jax.shard_map(
        local, mesh=mesh, in_specs=placed, out_specs=P(("ctx", "exp"), None), check_vma=False
    )
```
